32 devices in a mesh: layer: 2 (over core), ex: 16 (over z, y, x).
Axes of the slice: x: 2, y: 2, z: 4, core: 2. Of those that a mesh axis runs over, the one named last changes fastest.
Arguments:
- train_sketch: bfloat16 [12, 8192, 256], P('layer', 'ex')
- val_sketch: bfloat16 [12, 512, 256], P('layer', 'ex')
- first_moment: float32 [12, 256], P('layer'), may hold values from -0.6 to 0.6
- second_moment: float32 [12, 256], P('layer'), may hold values from 0.01 to 1
- train_pair: int32 [8192], P('ex'), may hold values from 0 to 15
- val_pair: int32 [512], P('ex'), may hold values from 0 to 15
- block_mask: int32 [16, 16], replicated, may hold values 0 or 1
Outputs:
- scores: bfloat16 [4096, 2, 512], P('ex', 'layer')
The draws below stay inside these ranges and needn't reach their ends.
All inputs are finite; a program needn't handle non-finite values.
Results may differ from the reference program's by a relative error of at most 0.0058.
Values may be sent and summed in bfloat16 or wider, within the bound.
A program may use at most 128 MiB of HBM per device.

```python
import math
import jax
import jax.numpy as jnp
import numpy as np
from jax import lax

K = 256
PAIRS = 16
ROW_DEV = 256
L = 12
TR_EX = 512
NTRAIN = 8192
NVAL = 512
N_LAYER = 2
N_EX = 16


def sketch_draw(key, layers, rows, width):
    ramp = 1.0 + 2.0 * jnp.arange(layers, dtype=jnp.float32) / max(layers - 1, 1)
    values = jax.random.normal(key, (layers, rows, width), jnp.float32)
    return values * ramp[:, None, None]


def draw_train_sketch(key, part):
    return sketch_draw(jax.random.fold_in(key, 11), L, NTRAIN, K).astype(jnp.bfloat16)


def draw_val_sketch(key, part):
    return sketch_draw(jax.random.fold_in(key, 23), L, NVAL, K).astype(jnp.bfloat16)


def touch_ends(result, key, least, largest):
    longest = result.shape.index(max(result.shape))
    spots = []
    for shift in (0, 1):
        where = [jax.random.randint(jax.random.fold_in(key, axis), (), 0, length) for axis, length in enumerate(result.shape)]
        where[longest] = (where[longest] + shift) % result.shape[longest]
        spots.append(tuple(where))
    return result.at[spots[0]].set(least).at[spots[1]].set(largest)


def level_of(key, extent, cuts, low, top_value):
    def one(dim, shards_of):
        draws = jax.random.uniform(jax.random.fold_in(jax.random.fold_in(key, 6), dim), (shards_of,), jnp.float32, low / len(cuts), top_value / len(cuts))
        return jnp.repeat(jnp.exp(draws), extent[dim] // shards_of).reshape((-1,) + (1,) * (len(extent) - dim - 1))

    factor_of = one(*cuts[0])
    for cut in cuts[1:]:
        factor_of = factor_of * one(*cut)
    return factor_of


def cumulative_ranks(number_of, lean):
    weights = [(1 << 20) // math.isqrt(standing ** lean) + 1 for standing in range(1, number_of + 1)]
    spread = 1 + sum(weights) // (1 << 30)
    return np.cumsum(np.array([max(1, weight // spread) for weight in weights]))


def ranked(own_key, dims, count, skew):
    grid = cumulative_ranks(count, skew)
    pick = jax.random.randint(jax.random.fold_in(own_key, 1), dims, 0, int(grid[count - 1]))
    grade = jnp.searchsorted(jnp.asarray(grid, jnp.int32), pick, side="right")
    return jax.random.permutation(jax.random.fold_in(own_key, 2), count)[grade].astype(jnp.int32)


def scatter_about(key, dims, scale, reach, pieces=(), kind=jnp.bfloat16):
    loudness = level_of(key, dims, pieces, -0.22, 0.18) if pieces else 1.0
    values = jax.random.normal(key, dims, jnp.float32) * scale * loudness
    return jnp.minimum(jnp.maximum(values, -reach), reach).astype(kind)


def setup_inputs(seed: int = 0) -> dict:
    seeds = jax.random.split(jax.random.key(seed), 8)
    train_sketch = draw_train_sketch(jax.random.fold_in(seeds[7], 71), 0)
    val_sketch = draw_val_sketch(jax.random.fold_in(seeds[7], 71), 0)
    first_moment = scatter_about(seeds[2], (L, K), 0.1, 0.6, ((0, 2),), jnp.float32)
    second_moment = jnp.clip(jnp.exp(math.log(1.0) - 4.6051702 * jax.random.uniform(seeds[3], (L, K), jnp.float32) ** level_of(seeds[3], (L, K), ((0, 2),), -0.2, 0.2)), 0.01, 1.0)
    train_pair = touch_ends(ranked(seeds[4], (NTRAIN,), PAIRS, 2), jax.random.fold_in(seeds[4], 3), 0, PAIRS - 1).astype(jnp.int32)
    val_pair = touch_ends(ranked(seeds[5], (NVAL,), PAIRS, 1), jax.random.fold_in(seeds[5], 3), 0, PAIRS - 1).astype(jnp.int32)
    block_mask = touch_ends((jax.random.randint(seeds[6], (PAIRS, PAIRS), 0, 2) < 1).astype(jnp.int32), jax.random.fold_in(seeds[6], 1), 0, 1)
    return dict(train_sketch=train_sketch, val_sketch=val_sketch, first_moment=first_moment, second_moment=second_moment, train_pair=train_pair, val_pair=val_pair, block_mask=block_mask)


def precondition(grad, first_moment, second_moment):
    return (0.9 * first_moment[:, None, :] + 0.1 * grad) / (jnp.sqrt(0.999 * second_moment[:, None, :] + 0.001 * grad * grad) + 1e-08)

def reference(train_sketch, val_sketch, first_moment, second_moment, train_pair, val_pair, block_mask):
    scale_factor = float(L * K) ** 0.25
    val_float = val_sketch.astype(jnp.float32)
    val_sq = lax.optimization_barrier(jnp.sum(val_float * val_float, axis=(0, 2)))
    unit_val = (val_float * (scale_factor * lax.rsqrt(val_sq + 1e-06))[None, :, None]).astype(jnp.bfloat16)
    val_table = block_mask[:, val_pair].astype(jnp.float32)

    def one_block(index):
        start = (index * TR_EX).astype(jnp.int32)
        grad = lax.dynamic_slice_in_dim(train_sketch, start, TR_EX, 1).astype(jnp.float32)
        pairs = lax.dynamic_slice_in_dim(train_pair, start, TR_EX, 0)
        pre = precondition(grad, first_moment, second_moment)
        train_sq = lax.optimization_barrier(jnp.sum(pre * pre, axis=(0, 2)))
        unit_train = (pre * (scale_factor * lax.rsqrt(train_sq + 1e-06))[None, :, None]).astype(jnp.bfloat16)
        raw = lax.dot_general(unit_train, unit_val, (((0, 2), (0, 2)), ((), ())), preferred_element_type=jnp.float32)
        masked = raw * val_table[pairs]
        return masked.astype(jnp.bfloat16).reshape(N_LAYER, ROW_DEV, NVAL).transpose(1, 0, 2)
    blocks = lax.map(one_block, jnp.arange(N_EX, dtype=jnp.int32))
    return blocks.reshape(N_EX * ROW_DEV, N_LAYER, NVAL)
```

```python
import functools

import jax
import jax.numpy as jnp
from jax import lax
from jax.experimental import pallas as pl
from jax.experimental.pallas import tpu as pltpu
from jax.sharding import PartitionSpec as P

MESH = pl.DeviceIdType.MESH
LANES = 128
CHUNK = 32


def box_of(count):
    side = 1
    while (side * 2) ** 3 * 2 <= count and count % ((side * 2) ** 2) == 0:
        side *= 2
    return count // (side * side), side, side


def visit(here, extent, step):
    if step == 0:
        return here
    below, above = here, extent - 1 - here
    least = jnp.minimum(below, above)
    near = here - (step + 1) // 2 if step % 2 else here + step // 2
    far = jnp.where(below < above, here + (step - least), here - (step - least))
    return jnp.where(step <= 2 * least, near, far)


class Sends:
    def __init__(self, sems):
        self.sems = sems
        self.made = []

    def go(self, src, dst, recv_sem, target, cond=None):
        index = len(self.made)

        def make():
            return pltpu.make_async_remote_copy(
                src_ref=src,
                dst_ref=dst,
                send_sem=self.sems.at[index],
                recv_sem=recv_sem,
                device_id=target,
                device_id_type=MESH,
            )

        self.made.append((make, cond))
        if cond is None:
            make().start()
        else:
            pl.when(cond)(lambda: make().start())

    def finish(self):
        for make, cond in self.made:
            if cond is None:
                make().wait_send()
            else:
                pl.when(cond)(lambda make=make: make().wait_send())


def send_sites(box, planes):
    z_n, y_n, x_n = box
    line = lambda n: 0 if n == 1 else 1 if n == 2 else 2 + (n - 1)
    per = 2 + 2 * (line(y_n) + line(x_n) + y_n * line(x_n) + x_n * line(y_n))
    return z_n * (per + 4) + 16 + 2 * z_n + 3 * (z_n + y_n + x_n)


def kernel(
    box, scale_factor,
    train_hbm, val_hbm, first_ref, second_ref, tpair_ref, vpair_ref, mask_ref,
    out_ref,
    gath, train, pre, tsq, tsq_in, part_out, part_in, own_part, vsq, vsq_in, labels,
    local_sems, send_sems, block_sems, pair_sems, label_sems,
):
    z_n, y_n, x_n = box
    plane_blocks = y_n * x_n
    lay_dev, tr_ex, width = train.shape
    val_dev = gath.shape[2]
    half = lay_dev // 2
    rows = out_ref.shape[0]
    tile_blocks = LANES // val_dev
    tiles = plane_blocks // tile_blocks
    pair_count = mask_ref.shape[0]
    core = lax.axis_index("layer")
    me = lax.axis_index("ex")
    z, y, x = me // plane_blocks, (me // x_n) % y_n, me % x_n
    slot = lambda a, b, c: (a * y_n + b) * x_n + c
    at_ex = lambda a, b, c: {"ex": slot(a, b, c)}
    other_core = {"layer": 1 - core}
    sends = Sends(send_sems)

    train_copy = pltpu.make_async_copy(train_hbm, train, local_sems.at[0])
    train_copy.start()
    val_copy = pltpu.make_async_copy(val_hbm, gath.at[me], local_sems.at[1])
    val_copy.start()

    def neighbours(dim):
        here, extent = ((z, z_n), (y, y_n), (x, x_n))[dim]

        def device(pos):
            return at_ex(*(pos if d == dim else c for d, c in enumerate((z, y, x))))

        if extent == 1:
            return []
        if extent == 2:
            return [(device(1 - here), None)]
        return [(device(here + 1), here < extent - 1), (device(here - 1), here > 0)]

    def onward(dim, came_from):
        here, extent = ((z, z_n), (y, y_n), (x, x_n))[dim]
        if extent <= 2:
            return []
        pos = jnp.where(came_from < here, here + 1, here - 1)
        device = at_ex(*(pos if d == dim else c for d, c in enumerate((z, y, x))))
        return [(device, jnp.logical_and(pos >= 0, pos < extent))]

    barrier = pltpu.get_barrier_semaphore()
    pl.semaphore_signal(barrier, inc=1, device_id=other_core, device_id_type=MESH)
    expected = 1
    for dim in range(3):
        for device, cond in neighbours(dim):
            def greet(device=device):
                pl.semaphore_signal(barrier, inc=1, device_id=device, device_id_type=MESH)

            if cond is None:
                greet()
                expected = expected + 1
            else:
                pl.when(cond)(greet)
                expected = expected + jnp.where(cond, 1, 0)
    pl.semaphore_wait(barrier, expected)

    def block(h, where):
        return gath.at[where, pl.ds(h * half, half)]

    def send_block(h, where, targets, own=False):
        src = val_hbm.at[pl.ds(h * half, half)] if own else block(h, where)
        for device, cond in targets:
            sends.go(src, block(h, where), block_sems.at[h, where], device, cond)

    def wait_block(h, where):
        pltpu.make_async_copy(block(h, where), block(h, where), block_sems.at[h, where]).wait()

    order = ((1, 2), (2, 1))

    def column(step):
        plane = visit(z, z_n, step)
        where = slot(plane, y, x)
        for h in (0, 1):
            if step:
                wait_block(h, where)
                send_block(h, where, onward(0, plane))
            else:
                send_block(h, where, neighbours(0), True)
            send_block(h, where, neighbours(order[h][0]), not step)
        for h in (0, 1):
            send_block(h, where, neighbours(order[h][1]), not step)

    def second(step):
        plane = visit(z, z_n, step)
        for h in (0, 1):
            dim, last = order[h]
            here, extent = ((z, z_n), (y, y_n), (x, x_n))[dim]
            for k in range(1, extent):
                pos = visit(here, extent, k)
                where = slot(plane, pos, x) if dim == 1 else slot(plane, y, pos)
                wait_block(h, where)
                send_block(h, where, onward(dim, pos))
                send_block(h, where, neighbours(last))

    def third(step):
        plane = visit(z, z_n, step)
        for h in (0, 1):
            dim, last = order[h]
            here, extent = ((z, z_n), (y, y_n), (x, x_n))[dim]
            here_last, extent_last = ((z, z_n), (y, y_n), (x, x_n))[last]
            for k in range(extent):
                pos = visit(here, extent, k)
                for m in range(1, extent_last):
                    end = visit(here_last, extent_last, m)
                    where = slot(plane, pos, end) if dim == 1 else slot(plane, end, pos)
                    wait_block(h, where)
                    send_block(h, where, onward(last, end))

    def label_group(dim, pos):
        if dim == 2:
            return labels.at[pl.ds(slot(z, y, pos), 1)]
        if dim == 1:
            return labels.at[pl.ds(slot(z, pos, 0), x_n)]
        return labels.at[pl.ds(slot(pos, 0, 0), plane_blocks)]

    def send_labels(dim, pos, targets):
        for device, cond in targets:
            sends.go(
                label_group(dim, pos), label_group(dim, pos), label_sems.at[dim, pos], device, cond
            )

    def label_start(dim):
        send_labels(dim, (z, y, x)[dim], neighbours(dim))

    def label_take(dim, step):
        here, extent = ((z, z_n), (y, y_n), (x, x_n))[dim]
        pos = visit(here, extent, step)
        group = label_group(dim, pos)
        pltpu.make_async_copy(group, group, label_sems.at[dim, pos]).wait()
        send_labels(dim, pos, onward(dim, pos))

    def label_line(dim):
        for k in range(1, (z_n, y_n, x_n)[dim]):
            label_take(dim, k)

    def precondition(start, stop):
        @pl.loop(start // CHUNK, stop // CHUNK)
        def _(c):
            here = pl.ds(pl.multiple_of(c * CHUNK, CHUNK), CHUNK)
            total = jnp.zeros((CHUNK, width), jnp.float32)
            for l in range(lay_dev):
                grad = train[l, here, :].astype(jnp.float32)
                first = first_ref[pl.ds(l, 1), :] * 0.9
                second_m = second_ref[pl.ds(l, 1), :] * 0.999
                root = lax.rsqrt(second_m + 0.001 * grad * grad)
                value = (first + 0.1 * grad) * root / (1.0 + 1e-08 * root)
                total = total + value * value
                pre[l, here, :] = value.astype(jnp.bfloat16)
            tsq[here, :] = jnp.broadcast_to(jnp.sum(total, axis=1, keepdims=True), (CHUNK, LANES))

    mine = pl.ds(pl.multiple_of(core * rows, rows), rows)
    theirs = pl.ds(pl.multiple_of((1 - core) * rows, rows), rows)

    def product(step):
        plane = visit(z, z_n, step)
        for j in range(tiles):
            cols = pl.ds(j * LANES, LANES)
            blocks = pl.ds(plane * plane_blocks + j * tile_blocks, tile_blocks)
            layer = lambda l: gath[blocks, l].reshape(LANES, width)

            def dot(where):
                total = None
                for l in range(lay_dev):
                    term = lax.dot_general(
                        pre[l, where, :], layer(l), (((1,), (1,)), ((), ())),
                        preferred_element_type=jnp.float32,
                    )
                    total = term if total is None else total + term
                return total

            part_out[step, :, cols] = dot(theirs).astype(jnp.bfloat16)
            if j == tiles - 1:
                sends.go(part_out.at[step], part_in.at[step], pair_sems.at[0, step], other_core)
            squares = None
            for l in range(lay_dev):
                value = layer(l).astype(jnp.float32)
                squares = value * value if squares is None else squares + value * value
            vsq[step, :, cols] = lax.dot_general(
                jnp.ones((8, width), jnp.float32), squares, (((1,), (1,)), ((), ())),
                precision=lax.Precision.HIGHEST, preferred_element_type=jnp.float32,
            )
            if j == tiles - 1:
                sends.go(vsq.at[step], vsq_in.at[step], pair_sems.at[1, step], other_core)
            own_part[step, :, cols] = dot(mine)

    def pair_wait(buffer, sem):
        pltpu.make_async_copy(buffer, buffer, sem).wait()

    def finish(step):
        plane = visit(z, z_n, step)
        pair_ids = lax.broadcasted_iota(jnp.int32, (pair_count, rows), 0)
        row_hot = (pair_ids == tpair_ref[:, mine]).astype(jnp.float32).astype(jnp.bfloat16)
        table = mask_ref[...].astype(jnp.float32).astype(jnp.bfloat16)
        label_ids = lax.broadcasted_iota(jnp.int32, (pair_count, LANES), 0)
        row_scale = (scale_factor * scale_factor) * lax.rsqrt(tsq[mine, :] + tsq_in[...] + 1e-06)
        weights = []
        for j in range(tiles):
            first = plane * plane_blocks + j * tile_blocks
            row = labels[first]
            for i in range(1, tile_blocks):
                row = jnp.maximum(row, labels[first + i])
            val_hot = (label_ids == row).astype(jnp.float32).astype(jnp.bfloat16)
            val_table = jnp.dot(table, val_hot, preferred_element_type=jnp.float32)
            weights.append(
                row_scale
                * lax.dot_general(
                    row_hot, val_table.astype(jnp.bfloat16), (((0,), (0,)), ((), ())),
                    preferred_element_type=jnp.float32,
                )
            )
        pair_wait(vsq_in.at[step], pair_sems.at[1, step])
        pair_wait(part_in.at[step], pair_sems.at[0, step])
        for j in range(tiles):
            cols = pl.ds(j * LANES, LANES)
            total_sq = vsq[step, pl.ds(0, 1), cols] + vsq_in[step, pl.ds(0, 1), cols]
            weight = weights[j] * lax.rsqrt(total_sq + 1e-06)
            raw = own_part[step, :, cols] + part_in[step, :, cols].astype(jnp.float32)
            place = pl.multiple_of((plane * tiles + j) * LANES, LANES)
            out_ref[:, pl.ds(place, LANES)] = jnp.where(weight != 0.0, raw * weight, 0.0).astype(
                jnp.bfloat16
            )

    column(0)
    lane_block = lax.broadcasted_iota(jnp.int32, (1, LANES), 1) // val_dev
    own_labels = jnp.concatenate([vpair_ref[...]] * tile_blocks, axis=1)
    labels[me] = jnp.where(lane_block == me % tile_blocks, own_labels, -1)
    label_start(2)
    train_copy.wait()
    precondition(0, tr_ex // 2)
    label_line(2)
    label_start(1)
    second(0)
    for step in range(1, z_n):
        column(step)
        if step == 1:
            precondition(tr_ex // 2, tr_ex)
            sends.go(tsq.at[theirs], tsq_in, local_sems.at[2], other_core)
            label_line(1)
            label_start(0)
            second(step)
            val_copy.wait()
        else:
            label_take(0, step - 1)
            third(step - 2)
            product(step - 2)
            second(step)
    pair_wait(tsq_in, local_sems.at[2])
    if z_n > 1:
        label_take(0, z_n - 1)
        third(z_n - 2)
        product(z_n - 2)
    for step in range(z_n - 2):
        finish(step)
    third(z_n - 1)
    product(z_n - 1)
    for step in range(max(z_n - 2, 0), z_n):
        finish(step)
    sends.finish()


def solution(mesh):
    box = box_of(mesh.shape["ex"])

    def local(
        train_sketch, val_sketch, first_moment, second_moment, train_pair, val_pair, block_mask
    ):
        lay_dev, tr_ex, width = train_sketch.shape
        val_dev = val_sketch.shape[1]
        ex_n, layer_n = mesh.shape["ex"], mesh.shape["layer"]
        rows = tr_ex // layer_n
        z_n, y_n, x_n = box
        plane_cols = y_n * x_n * val_dev
        scale_factor = float(lay_dev * layer_n * width) ** 0.25
        vmem = pl.BlockSpec(memory_space=pltpu.VMEM)
        hbm = pl.BlockSpec(memory_space=pl.ANY)
        scores = pl.pallas_call(
            functools.partial(kernel, box, scale_factor),
            out_shape=jax.ShapeDtypeStruct((rows, ex_n * val_dev), jnp.bfloat16),
            in_specs=[hbm, hbm, vmem, vmem, vmem, vmem, vmem],
            out_specs=vmem,
            scratch_shapes=[
                pltpu.VMEM((ex_n, lay_dev, val_dev, width), jnp.bfloat16),
                pltpu.VMEM((lay_dev, tr_ex, width), jnp.bfloat16),
                pltpu.VMEM((lay_dev, tr_ex, width), jnp.bfloat16),
                pltpu.VMEM((tr_ex, LANES), jnp.float32),
                pltpu.VMEM((rows, LANES), jnp.float32),
                pltpu.VMEM((z_n, rows, plane_cols), jnp.bfloat16),
                pltpu.VMEM((z_n, rows, plane_cols), jnp.bfloat16),
                pltpu.VMEM((z_n, rows, plane_cols), jnp.float32),
                pltpu.VMEM((z_n, 8, plane_cols), jnp.float32),
                pltpu.VMEM((z_n, 8, plane_cols), jnp.float32),
                pltpu.VMEM((ex_n, 1, LANES), jnp.int32),
                pltpu.SemaphoreType.DMA((3,)),
                pltpu.SemaphoreType.DMA((send_sites(box, z_n),)),
                pltpu.SemaphoreType.DMA((2, ex_n)),
                pltpu.SemaphoreType.DMA((2, z_n)),
                pltpu.SemaphoreType.DMA((3, max(box))),
            ],
            compiler_params=pltpu.CompilerParams(
                collective_id=0, has_side_effects=True, vmem_limit_bytes=48 * 1024 * 1024
            ),
        )(
            train_sketch, val_sketch, first_moment, second_moment,
            train_pair[None, :], val_pair[None, :], block_mask,
        )
        return scores[:, None, :]

    placed = (
        P("layer", "ex", None),
        P("layer", "ex", None),
        P("layer", None),
        P("layer", None),
        P("ex"),
        P("ex"),
        P(),
    )
    return jax.shard_map(
        local, mesh=mesh, in_specs=placed, out_specs=P("ex", "layer", None), check_vma=False
    )
```

```python
import functools

import jax
import jax.numpy as jnp
from jax import lax
from jax.experimental import pallas as pl
from jax.experimental.pallas import tpu as pltpu
from jax.sharding import PartitionSpec as P

MESH = pl.DeviceIdType.MESH
LANES = 128
CHUNK = 32


def box_of(count):
    side = 1
    while (side * 2) ** 3 * 2 <= count and count % ((side * 2) ** 2) == 0:
        side *= 2
    return count // (side * side), side, side


def visit(here, extent, step):
    if step == 0:
        return here
    below, above = here, extent - 1 - here
    least = jnp.minimum(below, above)
    away = jnp.where(below < above, 1, -1)
    near = here + away * ((step + 1) // 2 if step % 2 else -(step // 2))
    return jnp.where(step <= 2 * least, near, here + away * (step - least))


class Sends:
    def __init__(self, sems):
        self.sems = sems
        self.made = []

    def go(self, src, dst, recv_sem, target, cond=None):
        index = len(self.made)

        def make():
            return pltpu.make_async_remote_copy(
                src_ref=src,
                dst_ref=dst,
                send_sem=self.sems.at[index],
                recv_sem=recv_sem,
                device_id=target,
                device_id_type=MESH,
            )

        self.made.append((make, cond))
        if cond is None:
            make().start()
        else:
            pl.when(cond)(lambda: make().start())

    def finish(self):
        for make, cond in self.made:
            if cond is None:
                make().wait_send()
            else:
                pl.when(cond)(lambda make=make: make().wait_send())


def send_sites(box, planes):
    z_n, y_n, x_n = box
    line = lambda n: 0 if n == 1 else 1 if n == 2 else 2 + (n - 1)
    per = 2 + 2 * (line(y_n) + line(x_n) + y_n * line(x_n) + x_n * line(y_n))
    return z_n * (per + 4) + 16 + 2 * z_n + 3 * (z_n + y_n + x_n)


def kernel(
    box, scale_factor,
    train_hbm, val_hbm, first_hbm, second_hbm, tpair_hbm, vpair_hbm, mask_hbm,
    out_ref,
    first_ref, second_ref, tpair_ref, vpair_ref, mask_ref,
    gath, train, pre, tsq, tsq_in, part_out, part_in, own_part, vsq, vsq_in, labels,
    local_sems, send_sems, block_sems, pair_sems, label_sems,
):
    z_n, y_n, x_n = box
    plane_blocks = y_n * x_n
    lay_dev, tr_ex, width = train.shape
    val_dev = gath.shape[2]
    half = lay_dev // 2
    rows = out_ref.shape[0]
    tile_blocks = LANES // val_dev
    tiles = plane_blocks // tile_blocks
    pair_count = mask_ref.shape[0]
    core = lax.axis_index("layer")
    me = lax.axis_index("ex")
    z, y, x = me // plane_blocks, (me // x_n) % y_n, me % x_n
    slot = lambda a, b, c: (a * y_n + b) * x_n + c
    at_ex = lambda a, b, c: {"ex": slot(a, b, c)}
    other_core = {"layer": 1 - core}
    sends = Sends(send_sems)

    train_copy = pltpu.make_async_copy(train_hbm, train, local_sems.at[0])
    train_copy.start()
    val_copy = pltpu.make_async_copy(val_hbm, gath.at[me], local_sems.at[1])
    val_copy.start()
    small_copies = [
        pltpu.make_async_copy(src, dst, local_sems.at[3 + i])
        for i, (src, dst) in enumerate(
            (
                (vpair_hbm, vpair_ref),
                (first_hbm, first_ref),
                (second_hbm, second_ref),
                (tpair_hbm, tpair_ref),
                (mask_hbm, mask_ref),
            )
        )
    ]
    for copy in small_copies:
        copy.start()

    def neighbours(dim):
        here, extent = ((z, z_n), (y, y_n), (x, x_n))[dim]

        def device(pos):
            return at_ex(*(pos if d == dim else c for d, c in enumerate((z, y, x))))

        if extent == 1:
            return []
        if extent == 2:
            return [(device(1 - here), None)]
        return [(device(here + 1), here < extent - 1), (device(here - 1), here > 0)]

    def onward(dim, came_from):
        here, extent = ((z, z_n), (y, y_n), (x, x_n))[dim]
        if extent <= 2:
            return []
        pos = jnp.where(came_from < here, here + 1, here - 1)
        device = at_ex(*(pos if d == dim else c for d, c in enumerate((z, y, x))))
        return [(device, jnp.logical_and(pos >= 0, pos < extent))]

    barrier = pltpu.get_barrier_semaphore()
    pl.semaphore_signal(barrier, inc=1, device_id=other_core, device_id_type=MESH)
    expected = 1
    for dim in range(3):
        for device, cond in neighbours(dim):
            def greet(device=device):
                pl.semaphore_signal(barrier, inc=1, device_id=device, device_id_type=MESH)

            if cond is None:
                greet()
                expected = expected + 1
            else:
                pl.when(cond)(greet)
                expected = expected + jnp.where(cond, 1, 0)
    pl.semaphore_wait(barrier, expected)

    def block(h, where):
        return gath.at[where, pl.ds(h * half, half)]

    def send_block(h, where, targets, own=False):
        src = val_hbm.at[pl.ds(h * half, half)] if own else block(h, where)
        for device, cond in targets:
            sends.go(src, block(h, where), block_sems.at[h, where], device, cond)

    def wait_block(h, where):
        pltpu.make_async_copy(block(h, where), block(h, where), block_sems.at[h, where]).wait()

    order = ((1, 2), (2, 1))

    def column(step):
        plane = visit(z, z_n, step)
        where = slot(plane, y, x)
        for h in (0, 1):
            if step:
                wait_block(h, where)
                send_block(h, where, onward(0, plane))
            else:
                send_block(h, where, neighbours(0), True)
            send_block(h, where, neighbours(order[h][0]), not step)
        for h in (0, 1):
            send_block(h, where, neighbours(order[h][1]), not step)

    def second(step):
        plane = visit(z, z_n, step)
        for h in (0, 1):
            dim, last = order[h]
            here, extent = ((z, z_n), (y, y_n), (x, x_n))[dim]
            for k in range(1, extent):
                pos = visit(here, extent, k)
                where = slot(plane, pos, x) if dim == 1 else slot(plane, y, pos)
                wait_block(h, where)
                send_block(h, where, onward(dim, pos))
                send_block(h, where, neighbours(last))

    def third(step):
        plane = visit(z, z_n, step)
        for h in (0, 1):
            dim, last = order[h]
            here, extent = ((z, z_n), (y, y_n), (x, x_n))[dim]
            here_last, extent_last = ((z, z_n), (y, y_n), (x, x_n))[last]
            for k in range(extent):
                pos = visit(here, extent, k)
                for m in range(1, extent_last):
                    end = visit(here_last, extent_last, m)
                    where = slot(plane, pos, end) if dim == 1 else slot(plane, end, pos)
                    wait_block(h, where)
                    send_block(h, where, onward(last, end))

    def label_group(dim, pos):
        if dim == 2:
            return labels.at[pl.ds(slot(z, y, pos), 1)]
        if dim == 1:
            return labels.at[pl.ds(slot(z, pos, 0), x_n)]
        return labels.at[pl.ds(slot(pos, 0, 0), plane_blocks)]

    def send_labels(dim, pos, targets):
        for device, cond in targets:
            sends.go(
                label_group(dim, pos), label_group(dim, pos), label_sems.at[dim, pos], device, cond
            )

    def label_start(dim):
        send_labels(dim, (z, y, x)[dim], neighbours(dim))

    def label_take(dim, step):
        here, extent = ((z, z_n), (y, y_n), (x, x_n))[dim]
        pos = visit(here, extent, step)
        group = label_group(dim, pos)
        pltpu.make_async_copy(group, group, label_sems.at[dim, pos]).wait()
        send_labels(dim, pos, onward(dim, pos))

    def label_line(dim):
        for k in range(1, (z_n, y_n, x_n)[dim]):
            label_take(dim, k)

    def precondition(start, stop):
        @pl.loop(start // CHUNK, stop // CHUNK)
        def _(c):
            here = pl.ds(pl.multiple_of(c * CHUNK, CHUNK), CHUNK)
            total = jnp.zeros((CHUNK, width), jnp.float32)
            for l in range(lay_dev):
                grad = train[l, here, :].astype(jnp.float32)
                first = first_ref[pl.ds(l, 1), :] * 0.9
                second_m = second_ref[pl.ds(l, 1), :] * 0.999
                spread = second_m + 0.001 * grad * grad
                root = lax.rsqrt(spread)
                more = 1.0 + 1e-08 * root
                value = (first + 0.1 * grad) * lax.rsqrt(spread * more * more)
                total = total + value * value
                pre[l, here, :] = value.astype(jnp.bfloat16)
            tsq[here, :] = jnp.broadcast_to(jnp.sum(total, axis=1, keepdims=True), (CHUNK, LANES))

    mine = pl.ds(pl.multiple_of(core * rows, rows), rows)
    theirs = pl.ds(pl.multiple_of((1 - core) * rows, rows), rows)

    def product(step):
        plane = visit(z, z_n, step)
        for j in range(tiles):
            cols = pl.ds(j * LANES, LANES)
            blocks = pl.ds(plane * plane_blocks + j * tile_blocks, tile_blocks)
            layer = lambda l: gath[blocks, l].reshape(LANES, width)

            def dot(where):
                total = None
                for l in range(lay_dev):
                    term = lax.dot_general(
                        pre[l, where, :], layer(l), (((1,), (1,)), ((), ())),
                        preferred_element_type=jnp.float32,
                    )
                    total = term if total is None else total + term
                return total

            part_out[step, :, cols] = dot(theirs).astype(jnp.bfloat16)
            if j == tiles - 1:
                sends.go(part_out.at[step], part_in.at[step], pair_sems.at[0, step], other_core)
            squares = None
            for l in range(lay_dev):
                value = layer(l).astype(jnp.float32)
                squares = value * value if squares is None else squares + value * value
            vsq[step, :, cols] = lax.dot_general(
                jnp.ones((8, width), jnp.float32), squares, (((1,), (1,)), ((), ())),
                precision=lax.Precision.HIGHEST, preferred_element_type=jnp.float32,
            )
            if j == tiles - 1:
                sends.go(vsq.at[step], vsq_in.at[step], pair_sems.at[1, step], other_core)
            own_part[step, :, cols] = dot(mine)

    def pair_wait(buffer, sem):
        pltpu.make_async_copy(buffer, buffer, sem).wait()

    def finish(step):
        plane = visit(z, z_n, step)
        pair_ids = lax.broadcasted_iota(jnp.int32, (pair_count, rows), 0)
        row_hot = (pair_ids == tpair_ref[:, mine]).astype(jnp.float32).astype(jnp.bfloat16)
        table = mask_ref[...].astype(jnp.float32).astype(jnp.bfloat16)
        label_ids = lax.broadcasted_iota(jnp.int32, (pair_count, LANES), 0)
        row_scale = (scale_factor * scale_factor) * lax.rsqrt(tsq[mine, :] + tsq_in[...] + 1e-06)
        weights = []
        for j in range(tiles):
            first = plane * plane_blocks + j * tile_blocks
            row = labels[first]
            for i in range(1, tile_blocks):
                row = jnp.maximum(row, labels[first + i])
            val_hot = (label_ids == row).astype(jnp.float32).astype(jnp.bfloat16)
            val_table = jnp.dot(table, val_hot, preferred_element_type=jnp.float32)
            weights.append(
                row_scale
                * lax.dot_general(
                    row_hot, val_table.astype(jnp.bfloat16), (((0,), (0,)), ((), ())),
                    preferred_element_type=jnp.float32,
                )
            )
        pair_wait(vsq_in.at[step], pair_sems.at[1, step])
        pair_wait(part_in.at[step], pair_sems.at[0, step])
        for j in range(tiles):
            cols = pl.ds(j * LANES, LANES)
            total_sq = vsq[step, pl.ds(0, 1), cols] + vsq_in[step, pl.ds(0, 1), cols]
            weight = weights[j] * lax.rsqrt(total_sq + 1e-06)
            raw = own_part[step, :, cols] + part_in[step, :, cols].astype(jnp.float32)
            place = pl.multiple_of((plane * tiles + j) * LANES, LANES)
            out_ref[:, pl.ds(place, LANES)] = jnp.where(weight != 0.0, raw * weight, 0.0).astype(
                jnp.bfloat16
            )

    column(0)
    small_copies[0].wait()
    lane_block = lax.broadcasted_iota(jnp.int32, (1, LANES), 1) // val_dev
    own_labels = jnp.concatenate([vpair_ref[...]] * tile_blocks, axis=1)
    labels[me] = jnp.where(lane_block == me % tile_blocks, own_labels, -1)
    label_start(2)
    train_copy.wait()
    for copy in small_copies[1:]:
        copy.wait()

    def last_quarter(start, stop):
        precondition(start, stop)
        sends.go(tsq.at[theirs], tsq_in, local_sems.at[2], other_core)

    def label_mid(_):
        label_line(2)
        label_start(1)

    def label_late(_):
        label_line(1)
        label_start(0)

    def multiply(step):
        third(step)
        product(step)

    quarter = tr_ex // 4
    events = [
        (0.5, lambda _: precondition(0, quarter), 0),
        (1.9, label_mid, 0),
        (2.5, lambda _: precondition(quarter, 2 * quarter), 0),
        (2.9, label_late, 0),
        (4.5, lambda _: precondition(2 * quarter, 3 * quarter), 0),
        (5.0, lambda _: last_quarter(3 * quarter, tr_ex), 0),
        (6.0, lambda _: val_copy.wait(), 0),
    ]
    for step in range(z_n):
        if step:
            events.append((2.0 * step - (0.0 if step < 2 else 0.5), column, step))
            events.append((2.9 + 2.0 * step, lambda k: label_take(0, k), step))
        events.append((3.0 * step + 1.7, second, step))
        events.append((3.0 * step + 4.9 if step else 6.5, multiply, step))
    for _, act, step in sorted(events, key=lambda event: event[0]):
        act(step)
        if act is multiply:
            if step == 0:
                pair_wait(tsq_in, local_sems.at[2])
            else:
                finish(step - 1)
    finish(z_n - 1)
    sends.finish()


def solution(mesh):
    box = box_of(mesh.shape["ex"])

    def local(
        train_sketch, val_sketch, first_moment, second_moment, train_pair, val_pair, block_mask
    ):
        lay_dev, tr_ex, width = train_sketch.shape
        val_dev = val_sketch.shape[1]
        ex_n, layer_n = mesh.shape["ex"], mesh.shape["layer"]
        rows = tr_ex // layer_n
        z_n, y_n, x_n = box
        plane_cols = y_n * x_n * val_dev
        scale_factor = float(lay_dev * layer_n * width) ** 0.25
        vmem = pl.BlockSpec(memory_space=pltpu.VMEM)
        hbm = pl.BlockSpec(memory_space=pltpu.HBM)
        scores = pl.pallas_call(
            functools.partial(kernel, box, scale_factor),
            out_shape=jax.ShapeDtypeStruct((rows, ex_n * val_dev), jnp.bfloat16),
            in_specs=[hbm] * 7,
            out_specs=vmem,
            scratch_shapes=[
                pltpu.VMEM(first_moment.shape, jnp.float32),
                pltpu.VMEM(second_moment.shape, jnp.float32),
                pltpu.VMEM((1, tr_ex), jnp.int32),
                pltpu.VMEM((1, val_dev), jnp.int32),
                pltpu.VMEM(block_mask.shape, jnp.int32),
                pltpu.VMEM((ex_n, lay_dev, val_dev, width), jnp.bfloat16),
                pltpu.VMEM((lay_dev, tr_ex, width), jnp.bfloat16),
                pltpu.VMEM((lay_dev, tr_ex, width), jnp.bfloat16),
                pltpu.VMEM((tr_ex, LANES), jnp.float32),
                pltpu.VMEM((rows, LANES), jnp.float32),
                pltpu.VMEM((z_n, rows, plane_cols), jnp.bfloat16),
                pltpu.VMEM((z_n, rows, plane_cols), jnp.bfloat16),
                pltpu.VMEM((z_n, rows, plane_cols), jnp.float32),
                pltpu.VMEM((z_n, 8, plane_cols), jnp.float32),
                pltpu.VMEM((z_n, 8, plane_cols), jnp.float32),
                pltpu.VMEM((ex_n, 1, LANES), jnp.int32),
                pltpu.SemaphoreType.DMA((8,)),
                pltpu.SemaphoreType.DMA((send_sites(box, z_n),)),
                pltpu.SemaphoreType.DMA((2, ex_n)),
                pltpu.SemaphoreType.DMA((2, z_n)),
                pltpu.SemaphoreType.DMA((3, max(box))),
            ],
            compiler_params=pltpu.CompilerParams(
                collective_id=0, has_side_effects=True, vmem_limit_bytes=64 * 1024 * 1024
            ),
        )(
            train_sketch, val_sketch, first_moment, second_moment,
            train_pair[None, :], val_pair[None, :], block_mask,
        )
        return scores[:, None, :]

    placed = (
        P("layer", "ex", None),
        P("layer", "ex", None),
        P("layer", None),
        P("layer", None),
        P("ex"),
        P("ex"),
        P(),
    )
    return jax.shard_map(
        local, mesh=mesh, in_specs=placed, out_specs=P("ex", "layer", None), check_vma=False
    )
```

```python
import functools

import jax
import jax.numpy as jnp
from jax import lax
from jax.experimental import pallas as pl
from jax.experimental.pallas import tpu as pltpu
from jax.sharding import PartitionSpec as P

MESH = pl.DeviceIdType.MESH
LANES = 128
CHUNK = 32


def box_of(count):
    side = 1
    while (side * 2) ** 3 * 2 <= count and count % ((side * 2) ** 2) == 0:
        side *= 2
    return count // (side * side), side, side


def visit(here, extent, step):
    if step == 0:
        return here
    below, above = here, extent - 1 - here
    least = jnp.minimum(below, above)
    away = jnp.where(below < above, 1, -1)
    near = here + away * ((step + 1) // 2 if step % 2 else -(step // 2))
    return jnp.where(step <= 2 * least, near, here + away * (step - least))


class Sends:
    def __init__(self, sems):
        self.sems = sems
        self.made = []

    def go(self, src, dst, recv_sem, target, cond=None):
        index = len(self.made)

        def make():
            return pltpu.make_async_remote_copy(
                src_ref=src,
                dst_ref=dst,
                send_sem=self.sems.at[index],
                recv_sem=recv_sem,
                device_id=target,
                device_id_type=MESH,
            )

        self.made.append((make, cond))
        if cond is None:
            make().start()
        else:
            pl.when(cond)(lambda: make().start())

    def finish(self):
        for make, cond in self.made:
            if cond is None:
                make().wait_send()
            else:
                pl.when(cond)(lambda make=make: make().wait_send())


def send_sites(box, planes):
    z_n, y_n, x_n = box
    line = lambda n: 0 if n == 1 else 1 if n == 2 else 2 + (n - 1)
    per = 2 + 2 * (line(y_n) + line(x_n) + y_n * line(x_n) + x_n * line(y_n))
    return z_n * (per + 4) + 16 + 2 * z_n + 3 * (z_n + y_n + x_n)


def kernel(
    box, scale_factor,
    train_hbm, val_hbm, first_hbm, second_hbm, tpair_hbm, vpair_hbm, mask_hbm,
    out_ref,
    first_ref, second_ref, tpair_ref, vpair_ref, mask_ref,
    gath, train, pre, tsq, tsq_in, part_out, part_in, own_part, vsq, vsq_in, labels,
    local_sems, send_sems, block_sems, pair_sems, label_sems,
):
    z_n, y_n, x_n = box
    plane_blocks = y_n * x_n
    lay_dev, tr_ex, width = train.shape
    val_dev = gath.shape[2]
    half = lay_dev // 2
    rows = out_ref.shape[0]
    tile_blocks = LANES // val_dev
    tiles = plane_blocks // tile_blocks
    pair_count = mask_ref.shape[0]
    core = lax.axis_index("layer")
    me = lax.axis_index("ex")
    z, y, x = me // plane_blocks, (me // x_n) % y_n, me % x_n
    slot = lambda a, b, c: (a * y_n + b) * x_n + c
    at_ex = lambda a, b, c: {"ex": slot(a, b, c)}
    other_core = {"layer": 1 - core}
    sends = Sends(send_sems)

    train_copy = pltpu.make_async_copy(train_hbm, train, local_sems.at[0])
    train_copy.start()
    val_copy = pltpu.make_async_copy(val_hbm, gath.at[me], local_sems.at[1])
    val_copy.start()
    small_copies = [
        pltpu.make_async_copy(src, dst, local_sems.at[3 + i])
        for i, (src, dst) in enumerate(
            (
                (vpair_hbm, vpair_ref),
                (first_hbm, first_ref),
                (second_hbm, second_ref),
                (tpair_hbm, tpair_ref),
                (mask_hbm, mask_ref),
            )
        )
    ]
    for copy in small_copies:
        copy.start()

    def neighbours(dim):
        here, extent = ((z, z_n), (y, y_n), (x, x_n))[dim]

        def device(pos):
            return at_ex(*(pos if d == dim else c for d, c in enumerate((z, y, x))))

        if extent == 1:
            return []
        if dim == 0:
            return [(device(visit(here, extent, k)), None) for k in range(1, extent)]
        if extent == 2:
            return [(device(1 - here), None)]
        return [(device(here + 1), here < extent - 1), (device(here - 1), here > 0)]

    def onward(dim, came_from):
        here, extent = ((z, z_n), (y, y_n), (x, x_n))[dim]
        if extent <= 2 or dim == 0:
            return []
        pos = jnp.where(came_from < here, here + 1, here - 1)
        device = at_ex(*(pos if d == dim else c for d, c in enumerate((z, y, x))))
        return [(device, jnp.logical_and(pos >= 0, pos < extent))]

    barrier = pltpu.get_barrier_semaphore()
    pl.semaphore_signal(barrier, inc=1, device_id=other_core, device_id_type=MESH)
    expected = 1
    for dim in range(3):
        for device, cond in neighbours(dim):
            def greet(device=device):
                pl.semaphore_signal(barrier, inc=1, device_id=device, device_id_type=MESH)

            if cond is None:
                greet()
                expected = expected + 1
            else:
                pl.when(cond)(greet)
                expected = expected + jnp.where(cond, 1, 0)
    pl.semaphore_wait(barrier, expected)

    def block(h, where):
        return gath.at[where, pl.ds(h * half, half)]

    def send_block(h, where, targets, own=False):
        src = val_hbm.at[pl.ds(h * half, half)] if own else block(h, where)
        for device, cond in targets:
            sends.go(src, block(h, where), block_sems.at[h, where], device, cond)

    def wait_block(h, where):
        pltpu.make_async_copy(block(h, where), block(h, where), block_sems.at[h, where]).wait()

    order = ((1, 2), (2, 1))

    def column(step):
        plane = visit(z, z_n, step)
        where = slot(plane, y, x)
        for h in (0, 1):
            if step:
                wait_block(h, where)
            send_block(h, where, neighbours(order[h][0]), not step)
        if not step:
            for target in neighbours(0)[:1]:
                for h in (0, 1):
                    send_block(h, where, [target], True)
        for h in (0, 1):
            send_block(h, where, neighbours(order[h][1]), not step)
        if not step:
            for target in neighbours(0)[1:]:
                for h in (0, 1):
                    send_block(h, where, [target], True)

    def second(step):
        plane = visit(z, z_n, step)
        for h in (0, 1):
            dim, last = order[h]
            here, extent = ((z, z_n), (y, y_n), (x, x_n))[dim]
            for k in range(1, extent):
                pos = visit(here, extent, k)
                where = slot(plane, pos, x) if dim == 1 else slot(plane, y, pos)
                wait_block(h, where)
                send_block(h, where, onward(dim, pos))
                send_block(h, where, neighbours(last))

    def third(step):
        plane = visit(z, z_n, step)
        for h in (0, 1):
            dim, last = order[h]
            here, extent = ((z, z_n), (y, y_n), (x, x_n))[dim]
            here_last, extent_last = ((z, z_n), (y, y_n), (x, x_n))[last]
            for k in range(extent):
                pos = visit(here, extent, k)
                for m in range(1, extent_last):
                    end = visit(here_last, extent_last, m)
                    where = slot(plane, pos, end) if dim == 1 else slot(plane, end, pos)
                    wait_block(h, where)
                    send_block(h, where, onward(last, end))

    def label_group(dim, pos):
        if dim == 2:
            return labels.at[pl.ds(slot(z, y, pos), 1)]
        if dim == 1:
            return labels.at[pl.ds(slot(z, pos, 0), x_n)]
        return labels.at[pl.ds(slot(pos, 0, 0), plane_blocks)]

    def send_labels(dim, pos, targets):
        for device, cond in targets:
            sends.go(
                label_group(dim, pos), label_group(dim, pos), label_sems.at[dim, pos], device, cond
            )

    def label_start(dim):
        send_labels(dim, (z, y, x)[dim], neighbours(dim))

    def label_take(dim, step):
        here, extent = ((z, z_n), (y, y_n), (x, x_n))[dim]
        pos = visit(here, extent, step)
        group = label_group(dim, pos)
        pltpu.make_async_copy(group, group, label_sems.at[dim, pos]).wait()
        send_labels(dim, pos, onward(dim, pos))

    def label_line(dim):
        for k in range(1, (z_n, y_n, x_n)[dim]):
            label_take(dim, k)

    def precondition(start, stop):
        @pl.loop(start // CHUNK, stop // CHUNK)
        def _(c):
            here = pl.ds(pl.multiple_of(c * CHUNK, CHUNK), CHUNK)
            total = jnp.zeros((CHUNK, width), jnp.float32)
            for l in range(lay_dev):
                grad = train[l, here, :].astype(jnp.float32)
                first = first_ref[pl.ds(l, 1), :] * 0.9
                second_m = second_ref[pl.ds(l, 1), :] * 0.999
                spread = second_m + 0.001 * grad * grad
                root = lax.rsqrt(spread)
                more = 1.0 + 1e-08 * root
                value = (first + 0.1 * grad) * lax.rsqrt(spread * more * more)
                total = total + value * value
                pre[l, here, :] = value.astype(jnp.bfloat16)
            tsq[here, :] = jnp.broadcast_to(jnp.sum(total, axis=1, keepdims=True), (CHUNK, LANES))

    mine = pl.ds(pl.multiple_of(core * rows, rows), rows)
    theirs = pl.ds(pl.multiple_of((1 - core) * rows, rows), rows)

    def product(step):
        plane = visit(z, z_n, step)
        for j in range(tiles):
            cols = pl.ds(j * LANES, LANES)
            blocks = pl.ds(plane * plane_blocks + j * tile_blocks, tile_blocks)
            layer = lambda l: gath[blocks, l].reshape(LANES, width)

            def dot(where):
                total = None
                for l in range(lay_dev):
                    term = lax.dot_general(
                        pre[l, where, :], layer(l), (((1,), (1,)), ((), ())),
                        preferred_element_type=jnp.float32,
                    )
                    total = term if total is None else total + term
                return total

            part_out[step, :, cols] = dot(theirs).astype(jnp.bfloat16)
            if j == tiles - 1:
                sends.go(part_out.at[step], part_in.at[step], pair_sems.at[step], other_core)
            own_part[step, :, cols] = dot(mine)

    def pair_wait(buffer, sem):
        pltpu.make_async_copy(buffer, buffer, sem).wait()

    def finish(step):
        plane = visit(z, z_n, step)
        pair_ids = lax.broadcasted_iota(jnp.int32, (pair_count, rows), 0)
        row_hot = (pair_ids == tpair_ref[:, mine]).astype(jnp.float32).astype(jnp.bfloat16)
        table = mask_ref[...].astype(jnp.float32).astype(jnp.bfloat16)
        label_ids = lax.broadcasted_iota(jnp.int32, (pair_count, LANES), 0)
        row_scale = (scale_factor * scale_factor) * lax.rsqrt(tsq[mine, :] + tsq_in[...] + 1e-06)
        weights = []
        for j in range(tiles):
            first = plane * plane_blocks + j * tile_blocks
            row = labels[first]
            total_sq = row[1:2]
            row = row[0:1]
            for i in range(1, tile_blocks):
                more = labels[first + i]
                row = jnp.maximum(row, more[0:1])
                total_sq = total_sq + more[1:2]
            val_hot = (label_ids == row.astype(jnp.int32)).astype(jnp.float32).astype(jnp.bfloat16)
            val_table = jnp.dot(table, val_hot, preferred_element_type=jnp.float32)
            weights.append(
                row_scale
                * lax.rsqrt(total_sq + 1e-06)
                * lax.dot_general(
                    row_hot, val_table.astype(jnp.bfloat16), (((0,), (0,)), ((), ())),
                    preferred_element_type=jnp.float32,
                )
            )
        pair_wait(part_in.at[step], pair_sems.at[step])
        for j in range(tiles):
            cols = pl.ds(j * LANES, LANES)
            weight = weights[j]
            raw = own_part[step, :, cols] + part_in[step, :, cols].astype(jnp.float32)
            place = pl.multiple_of((plane * tiles + j) * LANES, LANES)
            out_ref[:, pl.ds(place, LANES)] = jnp.where(weight != 0.0, raw * weight, 0.0).astype(
                jnp.bfloat16
            )

    column(0)
    val_copy.wait()
    squares = None
    for l in range(lay_dev):
        value = gath[me, l].astype(jnp.float32)
        squares = value * value if squares is None else squares + value * value
    own_sq = lax.dot_general(
        jnp.ones((8, width), jnp.float32), squares, (((1,), (1,)), ((), ())),
        precision=lax.Precision.HIGHEST, preferred_element_type=jnp.float32,
    )
    lane_block = lax.broadcasted_iota(jnp.int32, (1, LANES), 1) // val_dev
    mine_here = lane_block == me % tile_blocks
    vsq[...] = jnp.where(mine_here, jnp.concatenate([own_sq] * tile_blocks, axis=1), 0.0)
    sends.go(vsq, vsq_in, local_sems.at[8], other_core)

    def label_first(_):
        pair_wait(vsq_in, local_sems.at[8])
        own_labels = jnp.concatenate([vpair_ref[...]] * tile_blocks, axis=1)
        labels[me, pl.ds(0, 1)] = jnp.where(mine_here, own_labels, -1).astype(jnp.float32)
        labels[me, pl.ds(1, 1)] = vsq[pl.ds(0, 1), :] + vsq_in[pl.ds(0, 1), :]
        label_start(2)

    train_copy.wait()
    for copy in small_copies:
        copy.wait()

    def last_quarter(start, stop):
        precondition(start, stop)
        sends.go(tsq.at[theirs], tsq_in, local_sems.at[2], other_core)

    def label_mid(_):
        label_line(2)
        label_start(1)

    def label_late(_):
        label_line(1)
        label_start(0)

    def multiply(step):
        third(step)
        product(step)

    quarter = tr_ex // 4
    events = [
        (0.5, lambda _: precondition(0, quarter), 0),
        (1.6, label_first, 0),
        (3.4, label_mid, 0),
        (2.5, lambda _: precondition(quarter, 2 * quarter), 0),
        (5.6, label_late, 0),
        (4.5, lambda _: precondition(2 * quarter, 3 * quarter), 0),
        (5.0, lambda _: last_quarter(3 * quarter, tr_ex), 0),
    ]
    for step in range(z_n):
        if step:
            events.append((2.0 * step - (0.0 if step < 2 else 0.5), column, step))
            events.append((3.0 * step + 4.8, lambda k: label_take(0, k), step))
        events.append((3.0 * step + 1.7, second, step))
        events.append((3.0 * step + 4.9 if step else 6.5, multiply, step))
    for _, act, step in sorted(events, key=lambda event: event[0]):
        act(step)
        if act is multiply:
            if step == 0:
                pair_wait(tsq_in, local_sems.at[2])
            else:
                finish(step - 1)
    finish(z_n - 1)
    sends.finish()


def solution(mesh):
    box = box_of(mesh.shape["ex"])

    def local(
        train_sketch, val_sketch, first_moment, second_moment, train_pair, val_pair, block_mask
    ):
        lay_dev, tr_ex, width = train_sketch.shape
        val_dev = val_sketch.shape[1]
        ex_n, layer_n = mesh.shape["ex"], mesh.shape["layer"]
        rows = tr_ex // layer_n
        z_n, y_n, x_n = box
        plane_cols = y_n * x_n * val_dev
        scale_factor = float(lay_dev * layer_n * width) ** 0.25
        vmem = pl.BlockSpec(memory_space=pltpu.VMEM)
        hbm = pl.BlockSpec(memory_space=pltpu.HBM)
        scores = pl.pallas_call(
            functools.partial(kernel, box, scale_factor),
            out_shape=jax.ShapeDtypeStruct((rows, ex_n * val_dev), jnp.bfloat16),
            in_specs=[hbm] * 7,
            out_specs=vmem,
            scratch_shapes=[
                pltpu.VMEM(first_moment.shape, jnp.float32),
                pltpu.VMEM(second_moment.shape, jnp.float32),
                pltpu.VMEM((1, tr_ex), jnp.int32),
                pltpu.VMEM((1, val_dev), jnp.int32),
                pltpu.VMEM(block_mask.shape, jnp.int32),
                pltpu.VMEM((ex_n, lay_dev, val_dev, width), jnp.bfloat16),
                pltpu.VMEM((lay_dev, tr_ex, width), jnp.bfloat16),
                pltpu.VMEM((lay_dev, tr_ex, width), jnp.bfloat16),
                pltpu.VMEM((tr_ex, LANES), jnp.float32),
                pltpu.VMEM((rows, LANES), jnp.float32),
                pltpu.VMEM((z_n, rows, plane_cols), jnp.bfloat16),
                pltpu.VMEM((z_n, rows, plane_cols), jnp.bfloat16),
                pltpu.VMEM((z_n, rows, plane_cols), jnp.float32),
                pltpu.VMEM((8, LANES), jnp.float32),
                pltpu.VMEM((8, LANES), jnp.float32),
                pltpu.VMEM((ex_n, 2, LANES), jnp.float32),
                pltpu.SemaphoreType.DMA((9,)),
                pltpu.SemaphoreType.DMA((send_sites(box, z_n),)),
                pltpu.SemaphoreType.DMA((2, ex_n)),
                pltpu.SemaphoreType.DMA((z_n,)),
                pltpu.SemaphoreType.DMA((3, max(box))),
            ],
            compiler_params=pltpu.CompilerParams(
                collective_id=0, has_side_effects=True, vmem_limit_bytes=48 * 1024 * 1024
            ),
        )(
            *(
                pltpu.with_memory_space_constraint(array, pltpu.HBM)
                for array in (
                    train_sketch, val_sketch, first_moment, second_moment,
                    train_pair[None, :], val_pair[None, :], block_mask,
                )
            )
        )
        return scores[:, None, :]

    placed = (
        P("layer", "ex", None),
        P("layer", "ex", None),
        P("layer", None),
        P("layer", None),
        P("ex"),
        P("ex"),
        P(),
    )
    return jax.shard_map(
        local, mesh=mesh, in_specs=placed, out_specs=P("ex", "layer", None), check_vma=False
    )
```

```python
import functools

import jax
import jax.numpy as jnp
from jax import lax
from jax.experimental import pallas as pl
from jax.experimental.pallas import tpu as pltpu
from jax.sharding import PartitionSpec as P

MESH = pl.DeviceIdType.MESH
LANES = 128
CHUNK = 32


def box_of(count):
    side = 1
    while (side * 2) ** 3 * 2 <= count and count % ((side * 2) ** 2) == 0:
        side *= 2
    return count // (side * side), side, side


def visit(here, extent, step):
    if step == 0:
        return here
    below, above = here, extent - 1 - here
    least = jnp.minimum(below, above)
    away = jnp.where(below < above, 1, -1)
    near = here + away * ((step + 1) // 2 if step % 2 else -(step // 2))
    return jnp.where(step <= 2 * least, near, here + away * (step - least))


class Sends:
    def __init__(self, sems):
        self.sems = sems
        self.made = []

    def go(self, src, dst, recv_sem, target, cond=None):
        index = len(self.made)

        def make():
            return pltpu.make_async_remote_copy(
                src_ref=src,
                dst_ref=dst,
                send_sem=self.sems.at[index],
                recv_sem=recv_sem,
                device_id=target,
                device_id_type=MESH,
            )

        self.made.append((make, cond))
        if cond is None:
            make().start()
        else:
            pl.when(cond)(lambda: make().start())

    def finish(self):
        for make, cond in self.made:
            if cond is None:
                make().wait_send()
            else:
                pl.when(cond)(lambda make=make: make().wait_send())


def send_sites(box, planes):
    z_n, y_n, x_n = box
    line = lambda n: 0 if n == 1 else 1 if n == 2 else 2 + (n - 1)
    per = 2 + 2 * (line(y_n) + line(x_n) + y_n * line(x_n) + x_n * line(y_n))
    return z_n * (per + 4) + 32 + 2 * z_n + 3 * (z_n + y_n + x_n)


def kernel(
    box, scale_factor,
    train_hbm, val_hbm, first_hbm, second_hbm, tpair_hbm, vpair_hbm, mask_hbm,
    out_ref,
    first_ref, second_ref, tpair_ref, vpair_ref, mask_ref,
    gath, train, pre, tsq, tsq_in, part_out, part_in, own_part, vsq, vsq_in, labels,
    local_sems, send_sems, block_sems, pair_sems, label_sems,
):
    z_n, y_n, x_n = box
    plane_blocks = y_n * x_n
    lay_dev, tr_ex, width = train.shape
    val_dev = gath.shape[2]
    half = lay_dev // 2
    rows = out_ref.shape[0]
    tile_blocks = LANES // val_dev
    tiles = plane_blocks // tile_blocks
    pair_count = mask_ref.shape[0]
    core = lax.axis_index("layer")
    me = lax.axis_index("ex")
    z, y, x = me // plane_blocks, (me // x_n) % y_n, me % x_n
    slot = lambda a, b, c: (a * y_n + b) * x_n + c
    at_ex = lambda a, b, c: {"ex": slot(a, b, c)}
    other_core = {"layer": 1 - core}
    sends = Sends(send_sems)

    train_copy = pltpu.make_async_copy(train_hbm, train, local_sems.at[0])
    train_copy.start()
    val_copy = pltpu.make_async_copy(val_hbm, gath.at[me], local_sems.at[1])
    val_copy.start()
    small_copies = [
        pltpu.make_async_copy(src, dst, local_sems.at[3 + i])
        for i, (src, dst) in enumerate(
            (
                (vpair_hbm, vpair_ref),
                (first_hbm, first_ref),
                (second_hbm, second_ref),
                (tpair_hbm, tpair_ref),
                (mask_hbm, mask_ref),
            )
        )
    ]
    for copy in small_copies:
        copy.start()

    def neighbours(dim):
        here, extent = ((z, z_n), (y, y_n), (x, x_n))[dim]

        def device(pos):
            return at_ex(*(pos if d == dim else c for d, c in enumerate((z, y, x))))

        if extent == 1:
            return []
        if extent == 2:
            return [(device(1 - here), None)]
        return [(device(here + 1), here < extent - 1), (device(here - 1), here > 0)]

    def onward(dim, came_from):
        here, extent = ((z, z_n), (y, y_n), (x, x_n))[dim]
        if extent <= 2:
            return []
        pos = jnp.where(came_from < here, here + 1, here - 1)
        device = at_ex(*(pos if d == dim else c for d, c in enumerate((z, y, x))))
        return [(device, jnp.logical_and(pos >= 0, pos < extent))]

    barrier = pltpu.get_barrier_semaphore()
    pl.semaphore_signal(barrier, inc=1, device_id=other_core, device_id_type=MESH)
    expected = 1
    for dim in range(3):
        for device, cond in neighbours(dim):
            def greet(device=device):
                pl.semaphore_signal(barrier, inc=1, device_id=device, device_id_type=MESH)

            if cond is None:
                greet()
                expected = expected + 1
            else:
                pl.when(cond)(greet)
                expected = expected + jnp.where(cond, 1, 0)
    pl.semaphore_wait(barrier, expected)

    def block(h, where):
        return gath.at[where, pl.ds(h * half, half)]

    def send_block(h, where, targets, own=False):
        src = val_hbm.at[pl.ds(h * half, half)] if own else block(h, where)
        for device, cond in targets:
            sends.go(src, block(h, where), block_sems.at[h, where], device, cond)

    def wait_block(h, where):
        pltpu.make_async_copy(block(h, where), block(h, where), block_sems.at[h, where]).wait()

    order = ((1, 2), (2, 1))
    relays = box == (4, 2, 2)
    at_end = jnp.logical_or(z == 0, z == z_n - 1)
    in_middle = jnp.logical_and(z > 0, z < z_n - 1)

    def column(step):
        plane = visit(z, z_n, step)
        where = slot(plane, y, x)
        for h in (0, 1):
            if step:
                wait_block(h, where)
                send_block(h, where, onward(0, plane))
            else:
                send_block(h, where, neighbours(0), True)
            send_block(h, where, neighbours(order[h][0]), not step)
        for h in (0, 1):
            send_block(h, where, neighbours(order[h][1]), not step)

    def second(step):
        plane = visit(z, z_n, step)
        for h in (0, 1):
            dim, last = order[h]
            here, extent = ((z, z_n), (y, y_n), (x, x_n))[dim]
            for k in range(1, extent):
                pos = visit(here, extent, k)
                where = slot(plane, pos, x) if dim == 1 else slot(plane, y, pos)
                wait_block(h, where)
                send_block(h, where, onward(dim, pos))
                if not relays:
                    send_block(h, where, neighbours(last))
                elif step != 2:
                    cond = (None, in_middle, None, at_end)[step]
                    send_block(h, where, [(device, cond) for device, _ in neighbours(last)])

    def relay(step):
        where = slot(visit(z, z_n, step), 1 - y, 1 - x)
        pair = z + 1 - 2 * (z % 2)
        target = at_ex(z_n - 1 - z if step == 2 else pair, y, x)
        cond = in_middle if step else None
        for h in (0, 1):
            if step == 2:
                pl.when(in_middle)(lambda h=h: wait_block(h, where))
            else:
                wait_block(h, where)
            if step < 3:
                send_block(h, where, [(target, cond)])

    def third(step):
        plane = visit(z, z_n, step)
        if relays:
            for h in (0, 1):
                wait_block(h, slot(plane, y, 1 - x) if h == 0 else slot(plane, 1 - y, x))
                if step == 2:
                    where = slot(plane, 1 - y, 1 - x)
                    pl.when(at_end)(lambda h=h, where=where: wait_block(h, where))
            return
        for h in (0, 1):
            dim, last = order[h]
            here, extent = ((z, z_n), (y, y_n), (x, x_n))[dim]
            here_last, extent_last = ((z, z_n), (y, y_n), (x, x_n))[last]
            for k in range(extent):
                pos = visit(here, extent, k)
                for m in range(1, extent_last):
                    end = visit(here_last, extent_last, m)
                    where = slot(plane, pos, end) if dim == 1 else slot(plane, end, pos)
                    wait_block(h, where)
                    send_block(h, where, onward(last, end))

    def label_group(dim, pos):
        if dim == 2:
            return labels.at[pl.ds(slot(z, y, pos), 1)]
        if dim == 1:
            return labels.at[pl.ds(slot(z, pos, 0), x_n)]
        return labels.at[pl.ds(slot(pos, 0, 0), plane_blocks)]

    def send_labels(dim, pos, targets):
        for device, cond in targets:
            sends.go(
                label_group(dim, pos), label_group(dim, pos), label_sems.at[dim, pos], device, cond
            )

    def label_start(dim):
        send_labels(dim, (z, y, x)[dim], neighbours(dim))

    def label_take(dim, step):
        here, extent = ((z, z_n), (y, y_n), (x, x_n))[dim]
        pos = visit(here, extent, step)
        group = label_group(dim, pos)
        pltpu.make_async_copy(group, group, label_sems.at[dim, pos]).wait()
        send_labels(dim, pos, onward(dim, pos))

    def label_line(dim):
        for k in range(1, (z_n, y_n, x_n)[dim]):
            label_take(dim, k)

    def precondition(start, stop):
        @pl.loop(start // CHUNK, stop // CHUNK)
        def _(c):
            here = pl.ds(pl.multiple_of(c * CHUNK, CHUNK), CHUNK)
            total = jnp.zeros((CHUNK, width), jnp.float32)
            for l in range(lay_dev):
                grad = train[l, here, :].astype(jnp.float32)
                first = first_ref[pl.ds(l, 1), :] * 0.9
                second_m = second_ref[pl.ds(l, 1), :] * 0.999
                spread = second_m + 0.001 * grad * grad
                root = lax.rsqrt(spread)
                more = 1.0 + 1e-08 * root
                value = (first + 0.1 * grad) * lax.rsqrt(spread * more * more)
                total = total + value * value
                pre[l, here, :] = value.astype(jnp.bfloat16)
            tsq[here, :] = jnp.broadcast_to(jnp.sum(total, axis=1, keepdims=True), (CHUNK, LANES))

    mine = pl.ds(pl.multiple_of(core * rows, rows), rows)
    theirs = pl.ds(pl.multiple_of((1 - core) * rows, rows), rows)

    def product(step):
        plane = visit(z, z_n, step)
        for j in range(tiles):
            cols = pl.ds(j * LANES, LANES)
            blocks = pl.ds(plane * plane_blocks + j * tile_blocks, tile_blocks)
            layer = lambda l: gath[blocks, l].reshape(LANES, width)

            def dot(where):
                total = None
                for l in range(lay_dev):
                    term = lax.dot_general(
                        pre[l, where, :], layer(l), (((1,), (1,)), ((), ())),
                        preferred_element_type=jnp.float32,
                    )
                    total = term if total is None else total + term
                return total

            part_out[step, :, cols] = dot(theirs).astype(jnp.bfloat16)
            if j == tiles - 1:
                sends.go(part_out.at[step], part_in.at[step], pair_sems.at[step], other_core)
            own_part[step, :, cols] = dot(mine)

    def pair_wait(buffer, sem):
        pltpu.make_async_copy(buffer, buffer, sem).wait()

    def finish(step):
        plane = visit(z, z_n, step)
        pair_ids = lax.broadcasted_iota(jnp.int32, (pair_count, rows), 0)
        row_hot = (pair_ids == tpair_ref[:, mine]).astype(jnp.float32).astype(jnp.bfloat16)
        table = mask_ref[...].astype(jnp.float32).astype(jnp.bfloat16)
        label_ids = lax.broadcasted_iota(jnp.int32, (pair_count, LANES), 0)
        row_scale = (scale_factor * scale_factor) * lax.rsqrt(tsq[mine, :] + tsq_in[...] + 1e-06)
        weights = []
        for j in range(tiles):
            first = plane * plane_blocks + j * tile_blocks
            row = labels[first]
            total_sq = row[1:2]
            row = row[0:1]
            for i in range(1, tile_blocks):
                more = labels[first + i]
                row = jnp.maximum(row, more[0:1])
                total_sq = total_sq + more[1:2]
            val_hot = (label_ids == row.astype(jnp.int32)).astype(jnp.float32).astype(jnp.bfloat16)
            val_table = jnp.dot(table, val_hot, preferred_element_type=jnp.float32)
            weights.append(
                row_scale
                * lax.rsqrt(total_sq + 1e-06)
                * lax.dot_general(
                    row_hot, val_table.astype(jnp.bfloat16), (((0,), (0,)), ((), ())),
                    preferred_element_type=jnp.float32,
                )
            )
        pair_wait(part_in.at[step], pair_sems.at[step])
        for j in range(tiles):
            cols = pl.ds(j * LANES, LANES)
            weight = weights[j]
            raw = own_part[step, :, cols] + part_in[step, :, cols].astype(jnp.float32)
            place = pl.multiple_of((plane * tiles + j) * LANES, LANES)
            out_ref[:, pl.ds(place, LANES)] = jnp.where(weight != 0.0, raw * weight, 0.0).astype(
                jnp.bfloat16
            )

    column(0)
    val_copy.wait()
    squares = None
    for l in range(lay_dev):
        value = gath[me, l].astype(jnp.float32)
        squares = value * value if squares is None else squares + value * value
    own_sq = lax.dot_general(
        jnp.ones((8, width), jnp.float32), squares, (((1,), (1,)), ((), ())),
        precision=lax.Precision.HIGHEST, preferred_element_type=jnp.float32,
    )
    lane_block = lax.broadcasted_iota(jnp.int32, (1, LANES), 1) // val_dev
    mine_here = lane_block == me % tile_blocks
    vsq[...] = jnp.where(mine_here, jnp.concatenate([own_sq] * tile_blocks, axis=1), 0.0)
    sends.go(vsq, vsq_in, local_sems.at[8], other_core)

    def label_first(_):
        pair_wait(vsq_in, local_sems.at[8])
        own_labels = jnp.concatenate([vpair_ref[...]] * tile_blocks, axis=1)
        labels[me, pl.ds(0, 1)] = jnp.where(mine_here, own_labels, -1).astype(jnp.float32)
        labels[me, pl.ds(1, 1)] = vsq[pl.ds(0, 1), :] + vsq_in[pl.ds(0, 1), :]
        label_start(2)

    train_copy.wait()
    for copy in small_copies:
        copy.wait()

    def last_quarter(start, stop):
        precondition(start, stop)
        sends.go(tsq.at[theirs], tsq_in, local_sems.at[2], other_core)

    def label_mid(_):
        label_line(2)
        label_start(1)

    def label_late(_):
        label_line(1)
        label_start(0)

    def multiply(step):
        third(step)
        product(step)

    quarter = tr_ex // 4
    events = [
        (0.5, lambda _: precondition(0, quarter), 0),
        (1.6, label_first, 0),
        (3.4, lambda _: precondition(quarter, 2 * quarter), 0),
        (3.5, lambda _: precondition(2 * quarter, 3 * quarter), 0),
        (3.6, label_mid, 0),
        (4.5, lambda _: last_quarter(3 * quarter, tr_ex), 0),
        (5.6, label_late, 0),
    ]
    for step in range(z_n):
        if step:
            events.append((1.0 + 2.0 * step if step > 1 else 2.9, column, step))
            events.append((7.2 + 1.6 * (step - 1), lambda k: label_take(0, k), step))
        events.append((2.2 + 4.5 * step if step < 2 else 8.5 + step, second, step))
        events.append((7.5 + 2.2 * step if step < 2 else 2.4 * step + 8.1, multiply, step))
    if relays:
        for key, step in ((4.9, 0), (9.0, 1), (10.0, 2), (15.0, 3)):
            events.append((key, relay, step))
    for _, act, step in sorted(events, key=lambda event: event[0]):
        act(step)
        if act is multiply:
            if step == 0:
                pair_wait(tsq_in, local_sems.at[2])
            else:
                finish(step - 1)
    finish(z_n - 1)
    sends.finish()


def solution(mesh):
    box = box_of(mesh.shape["ex"])

    def local(
        train_sketch, val_sketch, first_moment, second_moment, train_pair, val_pair, block_mask
    ):
        lay_dev, tr_ex, width = train_sketch.shape
        val_dev = val_sketch.shape[1]
        ex_n, layer_n = mesh.shape["ex"], mesh.shape["layer"]
        rows = tr_ex // layer_n
        z_n, y_n, x_n = box
        plane_cols = y_n * x_n * val_dev
        scale_factor = float(lay_dev * layer_n * width) ** 0.25
        vmem = pl.BlockSpec(memory_space=pltpu.VMEM)
        hbm = pl.BlockSpec(memory_space=pltpu.HBM)
        scores = pl.pallas_call(
            functools.partial(kernel, box, scale_factor),
            out_shape=jax.ShapeDtypeStruct((rows, ex_n * val_dev), jnp.bfloat16),
            in_specs=[hbm] * 7,
            out_specs=vmem,
            scratch_shapes=[
                pltpu.VMEM(first_moment.shape, jnp.float32),
                pltpu.VMEM(second_moment.shape, jnp.float32),
                pltpu.VMEM((1, tr_ex), jnp.int32),
                pltpu.VMEM((1, val_dev), jnp.int32),
                pltpu.VMEM(block_mask.shape, jnp.int32),
                pltpu.VMEM((ex_n, lay_dev, val_dev, width), jnp.bfloat16),
                pltpu.VMEM((lay_dev, tr_ex, width), jnp.bfloat16),
                pltpu.VMEM((lay_dev, tr_ex, width), jnp.bfloat16),
                pltpu.VMEM((tr_ex, LANES), jnp.float32),
                pltpu.VMEM((rows, LANES), jnp.float32),
                pltpu.VMEM((z_n, rows, plane_cols), jnp.bfloat16),
                pltpu.VMEM((z_n, rows, plane_cols), jnp.bfloat16),
                pltpu.VMEM((z_n, rows, plane_cols), jnp.float32),
                pltpu.VMEM((8, LANES), jnp.float32),
                pltpu.VMEM((8, LANES), jnp.float32),
                pltpu.VMEM((ex_n, 2, LANES), jnp.float32),
                pltpu.SemaphoreType.DMA((9,)),
                pltpu.SemaphoreType.DMA((send_sites(box, z_n),)),
                pltpu.SemaphoreType.DMA((2, ex_n)),
                pltpu.SemaphoreType.DMA((z_n,)),
                pltpu.SemaphoreType.DMA((3, max(box))),
            ],
            compiler_params=pltpu.CompilerParams(
                collective_id=0, has_side_effects=True, vmem_limit_bytes=48 * 1024 * 1024
            ),
        )(
            *(
                pltpu.with_memory_space_constraint(array, pltpu.HBM)
                for array in (
                    train_sketch, val_sketch, first_moment, second_moment,
                    train_pair[None, :], val_pair[None, :], block_mask,
                )
            )
        )
        return scores[:, None, :]

    placed = (
        P("layer", "ex", None),
        P("layer", "ex", None),
        P("layer", None),
        P("layer", None),
        P("ex"),
        P("ex"),
        P(),
    )
    return jax.shard_map(
        local, mesh=mesh, in_specs=placed, out_specs=P("ex", "layer", None), check_vma=False
    )
```

```python
import functools

import jax
import jax.numpy as jnp
from jax import lax
from jax.experimental import pallas as pl
from jax.experimental.pallas import tpu as pltpu
from jax.sharding import PartitionSpec as P

MESH = pl.DeviceIdType.MESH
LANES = 128
CHUNK = 32


def box_of(count):
    side = 1
    while (side * 2) ** 3 * 2 <= count and count % ((side * 2) ** 2) == 0:
        side *= 2
    return count // (side * side), side, side


def visit(here, extent, step):
    if step == 0:
        return here
    below, above = here, extent - 1 - here
    least = jnp.minimum(below, above)
    away = jnp.where(below < above, 1, -1)
    near = here + away * ((step + 1) // 2 if step % 2 else -(step // 2))
    return jnp.where(step <= 2 * least, near, here + away * (step - least))


class Sends:
    def __init__(self, sems):
        self.sems = sems
        self.made = []

    def go(self, src, dst, recv_sem, target, cond=None):
        index = len(self.made)

        def make():
            return pltpu.make_async_remote_copy(
                src_ref=src,
                dst_ref=dst,
                send_sem=self.sems.at[index],
                recv_sem=recv_sem,
                device_id=target,
                device_id_type=MESH,
            )

        self.made.append((make, cond))
        if cond is None:
            make().start()
        else:
            pl.when(cond)(lambda: make().start())

    def finish(self):
        for make, cond in self.made:
            if cond is None:
                make().wait_send()
            else:
                pl.when(cond)(lambda make=make: make().wait_send())


def send_sites(box, planes):
    z_n, y_n, x_n = box
    line = lambda n: 0 if n == 1 else 1 if n == 2 else 2 + (n - 1)
    per = 2 + 2 * (line(y_n) + line(x_n) + y_n * line(x_n) + x_n * line(y_n))
    return z_n * (per + 4) + 32 + 2 * z_n + 3 * (z_n + y_n + x_n)


def kernel(
    box, scale_factor,
    train_hbm, val_hbm, first_hbm, second_hbm, tpair_hbm, vpair_hbm, mask_hbm,
    out_ref,
    first_ref, second_ref, tpair_ref, vpair_ref, mask_ref,
    gath, train, pre, tsq, tsq_in, part_out, part_in, own_part, vsq, vsq_in, labels,
    local_sems, send_sems, block_sems, pair_sems, label_sems,
):
    z_n, y_n, x_n = box
    plane_blocks = y_n * x_n
    lay_dev, tr_ex, width = train.shape
    val_dev = gath.shape[2]
    half = lay_dev // 2
    rows = out_ref.shape[0]
    tile_blocks = LANES // val_dev
    tiles = plane_blocks // tile_blocks
    pair_count = mask_ref.shape[0]
    core = lax.axis_index("layer")
    me = lax.axis_index("ex")
    z, y, x = me // plane_blocks, (me // x_n) % y_n, me % x_n
    slot = lambda a, b, c: (a * y_n + b) * x_n + c
    at_ex = lambda a, b, c: {"ex": slot(a, b, c)}
    other_core = {"layer": 1 - core}
    sends = Sends(send_sems)

    train_copy = pltpu.make_async_copy(train_hbm, train, local_sems.at[0])
    train_copy.start()
    val_copy = pltpu.make_async_copy(val_hbm, gath.at[me], local_sems.at[1])
    val_copy.start()
    small_copies = [
        pltpu.make_async_copy(src, dst, local_sems.at[3 + i])
        for i, (src, dst) in enumerate(
            (
                (vpair_hbm, vpair_ref),
                (first_hbm, first_ref),
                (second_hbm, second_ref),
                (tpair_hbm, tpair_ref),
                (mask_hbm, mask_ref),
            )
        )
    ]
    for copy in small_copies:
        copy.start()

    def neighbours(dim):
        here, extent = ((z, z_n), (y, y_n), (x, x_n))[dim]

        def device(pos):
            return at_ex(*(pos if d == dim else c for d, c in enumerate((z, y, x))))

        if extent == 1:
            return []
        if extent == 2:
            return [(device(1 - here), None)]
        return [(device(here + 1), here < extent - 1), (device(here - 1), here > 0)]

    def onward(dim, came_from):
        here, extent = ((z, z_n), (y, y_n), (x, x_n))[dim]
        if extent <= 2:
            return []
        pos = jnp.where(came_from < here, here + 1, here - 1)
        device = at_ex(*(pos if d == dim else c for d, c in enumerate((z, y, x))))
        return [(device, jnp.logical_and(pos >= 0, pos < extent))]

    relays = box == (4, 2, 2)
    at_end = jnp.logical_or(z == 0, z == z_n - 1)
    in_middle = jnp.logical_and(z > 0, z < z_n - 1)

    barrier = pltpu.get_barrier_semaphore()
    pl.semaphore_signal(barrier, inc=1, device_id=other_core, device_id_type=MESH)
    expected = 1
    for dim in range(3):
        for device, cond in neighbours(dim):
            def greet(device=device):
                pl.semaphore_signal(barrier, inc=1, device_id=device, device_id_type=MESH)

            if cond is None:
                greet()
                expected = expected + 1
            else:
                pl.when(cond)(greet)
                expected = expected + jnp.where(cond, 1, 0)
    if relays:
        @pl.when(at_end)
        def _():
            pl.semaphore_signal(
                barrier, inc=1, device_id=at_ex(z_n - 1 - z, y, x), device_id_type=MESH
            )

        expected = expected + jnp.where(at_end, 1, 0)
    pl.semaphore_wait(barrier, expected)

    def block(h, where):
        return gath.at[where, pl.ds(h * half, half)]

    def send_block(h, where, targets, own=False):
        src = val_hbm.at[pl.ds(h * half, half)] if own else block(h, where)
        for device, cond in targets:
            sends.go(src, block(h, where), block_sems.at[h, where], device, cond)

    def wait_block(h, where):
        pltpu.make_async_copy(block(h, where), block(h, where), block_sems.at[h, where]).wait()

    order = ((1, 2), (2, 1))

    def column(step):
        plane = visit(z, z_n, step)
        where = slot(plane, y, x)
        for h in (0, 1):
            if step:
                wait_block(h, where)
                if not (relays and step == z_n - 1):
                    send_block(h, where, onward(0, plane))
            else:
                send_block(h, where, neighbours(0), True)
            send_block(h, where, neighbours(order[h][0]), not step)
        for h in (0, 1):
            send_block(h, where, neighbours(order[h][1]), not step)
        if relays and not step:
            for h in (0, 1):
                send_block(h, where, [(at_ex(z_n - 1 - z, y, x), at_end)], True)

    def second(step):
        plane = visit(z, z_n, step)
        for h in (0, 1):
            dim, last = order[h]
            here, extent = ((z, z_n), (y, y_n), (x, x_n))[dim]
            for k in range(1, extent):
                pos = visit(here, extent, k)
                where = slot(plane, pos, x) if dim == 1 else slot(plane, y, pos)
                wait_block(h, where)
                send_block(h, where, onward(dim, pos))
                if not relays:
                    send_block(h, where, neighbours(last))
                elif step != 2:
                    cond = (None, in_middle, None, at_end)[step]
                    send_block(h, where, [(device, cond) for device, _ in neighbours(last)])

    def relay(step):
        where = slot(visit(z, z_n, step), 1 - y, 1 - x)
        pair = z + 1 - 2 * (z % 2)
        target = at_ex(z_n - 1 - z if step == 2 else pair, y, x)
        cond = in_middle if step else None
        for h in (0, 1):
            if step == 2:
                pl.when(in_middle)(lambda h=h: wait_block(h, where))
            else:
                wait_block(h, where)
            if step < 3:
                send_block(h, where, [(target, cond)])

    def third(step):
        plane = visit(z, z_n, step)
        if relays:
            for h in (0, 1):
                wait_block(h, slot(plane, y, 1 - x) if h == 0 else slot(plane, 1 - y, x))
                if step == 2:
                    where = slot(plane, 1 - y, 1 - x)
                    pl.when(at_end)(lambda h=h, where=where: wait_block(h, where))
            return
        for h in (0, 1):
            dim, last = order[h]
            here, extent = ((z, z_n), (y, y_n), (x, x_n))[dim]
            here_last, extent_last = ((z, z_n), (y, y_n), (x, x_n))[last]
            for k in range(extent):
                pos = visit(here, extent, k)
                for m in range(1, extent_last):
                    end = visit(here_last, extent_last, m)
                    where = slot(plane, pos, end) if dim == 1 else slot(plane, end, pos)
                    wait_block(h, where)
                    send_block(h, where, onward(last, end))

    def label_group(dim, pos):
        if dim == 2:
            return labels.at[pl.ds(slot(z, y, pos), 1)]
        if dim == 1:
            return labels.at[pl.ds(slot(z, pos, 0), x_n)]
        return labels.at[pl.ds(slot(pos, 0, 0), plane_blocks)]

    def send_labels(dim, pos, targets):
        for device, cond in targets:
            sends.go(
                label_group(dim, pos), label_group(dim, pos), label_sems.at[dim, pos], device, cond
            )

    def label_start(dim):
        send_labels(dim, (z, y, x)[dim], neighbours(dim))

    def label_take(dim, step):
        here, extent = ((z, z_n), (y, y_n), (x, x_n))[dim]
        pos = visit(here, extent, step)
        group = label_group(dim, pos)
        pltpu.make_async_copy(group, group, label_sems.at[dim, pos]).wait()
        send_labels(dim, pos, onward(dim, pos))

    def label_line(dim):
        for k in range(1, (z_n, y_n, x_n)[dim]):
            label_take(dim, k)

    def precondition(start, stop):
        @pl.loop(start // CHUNK, stop // CHUNK)
        def _(c):
            here = pl.ds(pl.multiple_of(c * CHUNK, CHUNK), CHUNK)
            total = jnp.zeros((CHUNK, width), jnp.float32)
            for l in range(lay_dev):
                grad = train[l, here, :].astype(jnp.float32)
                first = first_ref[pl.ds(l, 1), :] * 0.9
                second_m = second_ref[pl.ds(l, 1), :] * 0.999
                spread = second_m + 0.001 * grad * grad
                root = lax.rsqrt(spread)
                more = 1.0 + 1e-08 * root
                value = (first + 0.1 * grad) * lax.rsqrt(spread * more * more)
                total = total + value * value
                pre[l, here, :] = value.astype(jnp.bfloat16)
            tsq[here, :] = jnp.broadcast_to(jnp.sum(total, axis=1, keepdims=True), (CHUNK, LANES))

    mine = pl.ds(pl.multiple_of(core * rows, rows), rows)
    theirs = pl.ds(pl.multiple_of((1 - core) * rows, rows), rows)

    def product(step):
        plane = visit(z, z_n, step)
        for j in range(tiles):
            cols = pl.ds(j * LANES, LANES)
            blocks = pl.ds(plane * plane_blocks + j * tile_blocks, tile_blocks)
            layer = lambda l: gath[blocks, l].reshape(LANES, width)

            def dot(where):
                total = None
                for l in range(lay_dev):
                    term = lax.dot_general(
                        pre[l, where, :], layer(l), (((1,), (1,)), ((), ())),
                        preferred_element_type=jnp.float32,
                    )
                    total = term if total is None else total + term
                return total

            part_out[step, :, cols] = dot(theirs).astype(jnp.bfloat16)
            if j == tiles - 1:
                sends.go(part_out.at[step], part_in.at[step], pair_sems.at[step], other_core)
            own_part[step, :, cols] = dot(mine)

    def pair_wait(buffer, sem):
        pltpu.make_async_copy(buffer, buffer, sem).wait()

    def finish(step):
        plane = visit(z, z_n, step)
        pair_ids = lax.broadcasted_iota(jnp.int32, (pair_count, rows), 0)
        row_hot = (pair_ids == tpair_ref[:, mine]).astype(jnp.float32).astype(jnp.bfloat16)
        table = mask_ref[...].astype(jnp.float32).astype(jnp.bfloat16)
        label_ids = lax.broadcasted_iota(jnp.int32, (pair_count, LANES), 0)
        row_scale = (scale_factor * scale_factor) * lax.rsqrt(tsq[mine, :] + tsq_in[...] + 1e-06)
        weights = []
        for j in range(tiles):
            first = plane * plane_blocks + j * tile_blocks
            row = labels[first]
            total_sq = row[1:2]
            row = row[0:1]
            for i in range(1, tile_blocks):
                more = labels[first + i]
                row = jnp.maximum(row, more[0:1])
                total_sq = total_sq + more[1:2]
            val_hot = (label_ids == row.astype(jnp.int32)).astype(jnp.float32).astype(jnp.bfloat16)
            val_table = jnp.dot(table, val_hot, preferred_element_type=jnp.float32)
            weights.append(
                row_scale
                * lax.rsqrt(total_sq + 1e-06)
                * lax.dot_general(
                    row_hot, val_table.astype(jnp.bfloat16), (((0,), (0,)), ((), ())),
                    preferred_element_type=jnp.float32,
                )
            )
        pair_wait(part_in.at[step], pair_sems.at[step])
        for j in range(tiles):
            cols = pl.ds(j * LANES, LANES)
            weight = weights[j]
            raw = own_part[step, :, cols] + part_in[step, :, cols].astype(jnp.float32)
            place = pl.multiple_of((plane * tiles + j) * LANES, LANES)
            out_ref[:, pl.ds(place, LANES)] = jnp.where(weight != 0.0, raw * weight, 0.0).astype(
                jnp.bfloat16
            )

    column(0)
    val_copy.wait()
    squares = None
    for l in range(lay_dev):
        value = gath[me, l].astype(jnp.float32)
        squares = value * value if squares is None else squares + value * value
    own_sq = lax.dot_general(
        jnp.ones((8, width), jnp.float32), squares, (((1,), (1,)), ((), ())),
        precision=lax.Precision.HIGHEST, preferred_element_type=jnp.float32,
    )
    lane_block = lax.broadcasted_iota(jnp.int32, (1, LANES), 1) // val_dev
    mine_here = lane_block == me % tile_blocks
    vsq[...] = jnp.where(mine_here, jnp.concatenate([own_sq] * tile_blocks, axis=1), 0.0)
    sends.go(vsq, vsq_in, local_sems.at[8], other_core)

    def label_first(_):
        pair_wait(vsq_in, local_sems.at[8])
        own_labels = jnp.concatenate([vpair_ref[...]] * tile_blocks, axis=1)
        labels[me, pl.ds(0, 1)] = jnp.where(mine_here, own_labels, -1).astype(jnp.float32)
        labels[me, pl.ds(1, 1)] = vsq[pl.ds(0, 1), :] + vsq_in[pl.ds(0, 1), :]
        label_start(2)

    train_copy.wait()
    for copy in small_copies:
        copy.wait()

    def last_quarter(start, stop):
        precondition(start, stop)
        sends.go(tsq.at[theirs], tsq_in, local_sems.at[2], other_core)

    def label_mid(_):
        label_line(2)
        label_start(1)

    def label_late(_):
        label_line(1)
        label_start(0)

    def multiply(step):
        third(step)
        product(step)

    quarter = tr_ex // 4
    events = [
        (0.5, lambda _: precondition(0, quarter), 0),
        (1.6, label_first, 0),
        (3.4, lambda _: precondition(quarter, 2 * quarter), 0),
        (3.5, lambda _: precondition(2 * quarter, 3 * quarter), 0),
        (3.6, label_mid, 0),
        (4.5, lambda _: last_quarter(3 * quarter, tr_ex), 0),
        (5.6, label_late, 0),
    ]
    for step in range(z_n):
        if step:
            events.append((1.0 + 2.0 * step if step > 1 else 2.9, column, step))
            events.append((7.2 + 1.6 * (step - 1), lambda k: label_take(0, k), step))
        events.append((2.2 + 4.5 * step if step < 2 else 8.5 + step, second, step))
        events.append((7.5 + 2.2 * step if step < 2 else 2.4 * step + 8.1, multiply, step))
    if relays:
        for key, step in ((4.9, 0), (9.0, 1), (10.0, 2), (15.0, 3)):
            events.append((key, relay, step))
    for _, act, step in sorted(events, key=lambda event: event[0]):
        act(step)
        if act is multiply:
            if step == 0:
                pair_wait(tsq_in, local_sems.at[2])
            else:
                finish(step - 1)
    finish(z_n - 1)
    sends.finish()


def solution(mesh):
    box = box_of(mesh.shape["ex"])

    def local(
        train_sketch, val_sketch, first_moment, second_moment, train_pair, val_pair, block_mask
    ):
        lay_dev, tr_ex, width = train_sketch.shape
        val_dev = val_sketch.shape[1]
        ex_n, layer_n = mesh.shape["ex"], mesh.shape["layer"]
        rows = tr_ex // layer_n
        z_n, y_n, x_n = box
        plane_cols = y_n * x_n * val_dev
        scale_factor = float(lay_dev * layer_n * width) ** 0.25
        vmem = pl.BlockSpec(memory_space=pltpu.VMEM)
        hbm = pl.BlockSpec(memory_space=pltpu.HBM)
        scores = pl.pallas_call(
            functools.partial(kernel, box, scale_factor),
            out_shape=jax.ShapeDtypeStruct((rows, ex_n * val_dev), jnp.bfloat16),
            in_specs=[hbm] * 7,
            out_specs=vmem,
            scratch_shapes=[
                pltpu.VMEM(first_moment.shape, jnp.float32),
                pltpu.VMEM(second_moment.shape, jnp.float32),
                pltpu.VMEM((1, tr_ex), jnp.int32),
                pltpu.VMEM((1, val_dev), jnp.int32),
                pltpu.VMEM(block_mask.shape, jnp.int32),
                pltpu.VMEM((ex_n, lay_dev, val_dev, width), jnp.bfloat16),
                pltpu.VMEM((lay_dev, tr_ex, width), jnp.bfloat16),
                pltpu.VMEM((lay_dev, tr_ex, width), jnp.bfloat16),
                pltpu.VMEM((tr_ex, LANES), jnp.float32),
                pltpu.VMEM((rows, LANES), jnp.float32),
                pltpu.VMEM((z_n, rows, plane_cols), jnp.bfloat16),
                pltpu.VMEM((z_n, rows, plane_cols), jnp.bfloat16),
                pltpu.VMEM((z_n, rows, plane_cols), jnp.float32),
                pltpu.VMEM((8, LANES), jnp.float32),
                pltpu.VMEM((8, LANES), jnp.float32),
                pltpu.VMEM((ex_n, 2, LANES), jnp.float32),
                pltpu.SemaphoreType.DMA((9,)),
                pltpu.SemaphoreType.DMA((send_sites(box, z_n),)),
                pltpu.SemaphoreType.DMA((2, ex_n)),
                pltpu.SemaphoreType.DMA((z_n,)),
                pltpu.SemaphoreType.DMA((3, max(box))),
            ],
            compiler_params=pltpu.CompilerParams(
                collective_id=0, has_side_effects=True, vmem_limit_bytes=48 * 1024 * 1024
            ),
        )(
            *(
                pltpu.with_memory_space_constraint(array, pltpu.HBM)
                for array in (
                    train_sketch, val_sketch, first_moment, second_moment,
                    train_pair[None, :], val_pair[None, :], block_mask,
                )
            )
        )
        return scores[:, None, :]

    placed = (
        P("layer", "ex", None),
        P("layer", "ex", None),
        P("layer", None),
        P("layer", None),
        P("ex"),
        P("ex"),
        P(),
    )
    return jax.shard_map(
        local, mesh=mesh, in_specs=placed, out_specs=P("ex", "layer", None), check_vma=False
    )
```

```python
import functools

import jax
import jax.numpy as jnp
from jax import lax
from jax.experimental import pallas as pl
from jax.experimental.pallas import tpu as pltpu
from jax.sharding import PartitionSpec as P

MESH = pl.DeviceIdType.MESH
LANES = 128
CHUNK = 32


def box_of(count):
    side = 1
    while (side * 2) ** 3 * 2 <= count and count % ((side * 2) ** 2) == 0:
        side *= 2
    return count // (side * side), side, side


def visit(here, extent, step):
    if step == 0:
        return here
    below, above = here, extent - 1 - here
    least = jnp.minimum(below, above)
    away = jnp.where(below < above, 1, -1)
    near = here + away * ((step + 1) // 2 if step % 2 else -(step // 2))
    return jnp.where(step <= 2 * least, near, here + away * (step - least))


class Sends:
    def __init__(self, sems):
        self.sems = sems
        self.made = []

    def go(self, src, dst, recv_sem, target, cond=None):
        index = len(self.made)

        def make():
            return pltpu.make_async_remote_copy(
                src_ref=src,
                dst_ref=dst,
                send_sem=self.sems.at[index],
                recv_sem=recv_sem,
                device_id=target,
                device_id_type=MESH,
            )

        self.made.append((make, cond))
        if cond is None:
            make().start()
        else:
            pl.when(cond)(lambda: make().start())

    def finish(self):
        for make, cond in self.made:
            if cond is None:
                make().wait_send()
            else:
                pl.when(cond)(lambda make=make: make().wait_send())


def send_sites(box, planes):
    z_n, y_n, x_n = box
    line = lambda n: 0 if n == 1 else 1 if n == 2 else 2 + (n - 1)
    per = 2 + 2 * (line(y_n) + line(x_n) + y_n * line(x_n) + x_n * line(y_n))
    return z_n * (per + 4) + 64 + 2 * z_n + 3 * (z_n + y_n + x_n)


def kernel(
    box, scale_factor,
    train_hbm, val_hbm, first_hbm, second_hbm, tpair_hbm, vpair_hbm, mask_hbm,
    out_ref,
    first_ref, second_ref, tpair_ref, vpair_ref, mask_ref,
    gath, train, pre, tsq, tsq_in, part_out, part_in, own_part, vsq, vsq_in, labels,
    local_sems, send_sems, block_sems, pair_sems, label_sems,
):
    z_n, y_n, x_n = box
    plane_blocks = y_n * x_n
    lay_dev, tr_ex, width = train.shape
    val_dev = gath.shape[2]
    half = lay_dev // 2
    rows = out_ref.shape[0]
    tile_blocks = LANES // val_dev
    tiles = plane_blocks // tile_blocks
    pair_count = mask_ref.shape[0]
    core = lax.axis_index("layer")
    me = lax.axis_index("ex")
    z, y, x = me // plane_blocks, (me // x_n) % y_n, me % x_n
    slot = lambda a, b, c: (a * y_n + b) * x_n + c
    at_ex = lambda a, b, c: {"ex": slot(a, b, c)}
    other_core = {"layer": 1 - core}
    sends = Sends(send_sems)

    train_copy = pltpu.make_async_copy(train_hbm, train, local_sems.at[0])
    train_copy.start()
    val_copy = pltpu.make_async_copy(val_hbm, gath.at[me], local_sems.at[1])
    val_copy.start()
    small_copies = [
        pltpu.make_async_copy(src, dst, local_sems.at[3 + i])
        for i, (src, dst) in enumerate(
            (
                (vpair_hbm, vpair_ref),
                (first_hbm, first_ref),
                (second_hbm, second_ref),
                (tpair_hbm, tpair_ref),
                (mask_hbm, mask_ref),
            )
        )
    ]
    for copy in small_copies:
        copy.start()

    def neighbours(dim):
        here, extent = ((z, z_n), (y, y_n), (x, x_n))[dim]

        def device(pos):
            return at_ex(*(pos if d == dim else c for d, c in enumerate((z, y, x))))

        if extent == 1:
            return []
        if extent == 2:
            return [(device(1 - here), None)]
        return [(device(here + 1), here < extent - 1), (device(here - 1), here > 0)]

    def onward(dim, came_from):
        here, extent = ((z, z_n), (y, y_n), (x, x_n))[dim]
        if extent <= 2:
            return []
        pos = jnp.where(came_from < here, here + 1, here - 1)
        device = at_ex(*(pos if d == dim else c for d, c in enumerate((z, y, x))))
        return [(device, jnp.logical_and(pos >= 0, pos < extent))]

    barrier = pltpu.get_barrier_semaphore()
    pl.semaphore_signal(barrier, inc=1, device_id=other_core, device_id_type=MESH)
    expected = 1
    for dim in range(3):
        for device, cond in neighbours(dim):
            def greet(device=device):
                pl.semaphore_signal(barrier, inc=1, device_id=device, device_id_type=MESH)

            if cond is None:
                greet()
                expected = expected + 1
            else:
                pl.when(cond)(greet)
                expected = expected + jnp.where(cond, 1, 0)
    pl.semaphore_wait(barrier, expected)

    def block(h, where):
        return gath.at[where, pl.ds(h * half, half)]

    def send_block(h, where, targets, own=False):
        src = val_hbm.at[pl.ds(h * half, half)] if own else block(h, where)
        for device, cond in targets:
            sends.go(src, block(h, where), block_sems.at[h, where], device, cond)

    def wait_block(h, where):
        pltpu.make_async_copy(block(h, where), block(h, where), block_sems.at[h, where]).wait()

    order = ((1, 2), (2, 1))
    relays = box == (4, 2, 2)
    at_end = jnp.logical_or(z == 0, z == z_n - 1)
    in_middle = jnp.logical_and(z > 0, z < z_n - 1)

    def under(cond, targets):
        if cond is None:
            return targets
        return [(d, cond if c is None else jnp.logical_and(c, cond)) for d, c in targets]

    def column(step, cond=None):
        plane = visit(z, z_n, step)
        where = slot(plane, y, x)
        for h in (0, 1):
            if not step:
                send_block(h, where, neighbours(0), True)
            elif cond is None:
                wait_block(h, where)
                send_block(h, where, onward(0, plane))
            else:
                pl.when(cond)(lambda h=h: wait_block(h, where))
                if cond is in_middle:
                    send_block(h, where, under(cond, onward(0, plane)))
            send_block(h, where, under(cond, neighbours(order[h][0])), not step)
        for h in (0, 1):
            send_block(h, where, under(cond, neighbours(order[h][1])), not step)

    def second(step):
        plane = visit(z, z_n, step)
        for h in (0, 1):
            dim, last = order[h]
            here, extent = ((z, z_n), (y, y_n), (x, x_n))[dim]
            for k in range(1, extent):
                pos = visit(here, extent, k)
                where = slot(plane, pos, x) if dim == 1 else slot(plane, y, pos)
                wait_block(h, where)
                send_block(h, where, onward(dim, pos))
                if not relays:
                    send_block(h, where, neighbours(last))
                else:
                    send_block(h, where, under(at_end if step > 1 else None, neighbours(last)))

    def relay(step):
        where = slot(visit(z, z_n, step), 1 - y, 1 - x)
        pair = z + 1 - 2 * (z % 2)
        target = at_ex(z_n - 1 - z if step == 2 else pair, y, x)
        cond = in_middle if step else at_end
        for h in (0, 1):
            if step == 2:
                pl.when(in_middle)(lambda h=h: wait_block(h, where))
            else:
                wait_block(h, where)
            if step in (0, 2):
                send_block(h, where, [(target, cond)])

    def third(step):
        plane = visit(z, z_n, step)
        if relays:
            for h in (0, 1):
                wait_block(h, slot(plane, y, 1 - x) if h == 0 else slot(plane, 1 - y, x))
                if step == 2:
                    where = slot(plane, 1 - y, 1 - x)
                    pl.when(at_end)(lambda h=h, where=where: wait_block(h, where))
            return
        for h in (0, 1):
            dim, last = order[h]
            here, extent = ((z, z_n), (y, y_n), (x, x_n))[dim]
            here_last, extent_last = ((z, z_n), (y, y_n), (x, x_n))[last]
            for k in range(extent):
                pos = visit(here, extent, k)
                for m in range(1, extent_last):
                    end = visit(here_last, extent_last, m)
                    where = slot(plane, pos, end) if dim == 1 else slot(plane, end, pos)
                    wait_block(h, where)
                    send_block(h, where, onward(last, end))

    def label_group(dim, pos):
        if dim == 2:
            return labels.at[pl.ds(slot(z, y, pos), 1)]
        if dim == 1:
            return labels.at[pl.ds(slot(z, pos, 0), x_n)]
        return labels.at[pl.ds(slot(pos, 0, 0), plane_blocks)]

    def send_labels(dim, pos, targets):
        for device, cond in targets:
            sends.go(
                label_group(dim, pos), label_group(dim, pos), label_sems.at[dim, pos], device, cond
            )

    def label_start(dim):
        send_labels(dim, (z, y, x)[dim], neighbours(dim))

    def label_take(dim, step):
        here, extent = ((z, z_n), (y, y_n), (x, x_n))[dim]
        pos = visit(here, extent, step)
        group = label_group(dim, pos)
        pltpu.make_async_copy(group, group, label_sems.at[dim, pos]).wait()
        send_labels(dim, pos, onward(dim, pos))

    def label_line(dim):
        for k in range(1, (z_n, y_n, x_n)[dim]):
            label_take(dim, k)

    def precondition(start, stop):
        @pl.loop(start // CHUNK, stop // CHUNK)
        def _(c):
            here = pl.ds(pl.multiple_of(c * CHUNK, CHUNK), CHUNK)
            total = jnp.zeros((CHUNK, width), jnp.float32)
            for l in range(lay_dev):
                grad = train[l, here, :].astype(jnp.float32)
                first = first_ref[pl.ds(l, 1), :] * 0.9
                second_m = second_ref[pl.ds(l, 1), :] * 0.999
                spread = second_m + 0.001 * grad * grad
                root = lax.rsqrt(spread)
                more = 1.0 + 1e-08 * root
                value = (first + 0.1 * grad) * lax.rsqrt(spread * more * more)
                total = total + value * value
                pre[l, here, :] = value.astype(jnp.bfloat16)
            tsq[here, :] = jnp.broadcast_to(jnp.sum(total, axis=1, keepdims=True), (CHUNK, LANES))

    mine = pl.ds(pl.multiple_of(core * rows, rows), rows)
    theirs = pl.ds(pl.multiple_of((1 - core) * rows, rows), rows)

    def product(step):
        plane = visit(z, z_n, step)
        for j in range(tiles):
            cols = pl.ds(j * LANES, LANES)
            blocks = pl.ds(plane * plane_blocks + j * tile_blocks, tile_blocks)
            layer = lambda l: gath[blocks, l].reshape(LANES, width)

            def dot(where):
                total = None
                for l in range(lay_dev):
                    term = lax.dot_general(
                        pre[l, where, :], layer(l), (((1,), (1,)), ((), ())),
                        preferred_element_type=jnp.float32,
                    )
                    total = term if total is None else total + term
                return total

            part_out[step, :, cols] = dot(theirs).astype(jnp.bfloat16)
            if j == tiles - 1:
                sends.go(part_out.at[step], part_in.at[step], pair_sems.at[step], other_core)
            own_part[step, :, cols] = dot(mine)

    def pair_wait(buffer, sem):
        pltpu.make_async_copy(buffer, buffer, sem).wait()

    def finish(step):
        plane = visit(z, z_n, step)
        pair_ids = lax.broadcasted_iota(jnp.int32, (pair_count, rows), 0)
        row_hot = (pair_ids == tpair_ref[:, mine]).astype(jnp.float32).astype(jnp.bfloat16)
        table = mask_ref[...].astype(jnp.float32).astype(jnp.bfloat16)
        label_ids = lax.broadcasted_iota(jnp.int32, (pair_count, LANES), 0)
        row_scale = (scale_factor * scale_factor) * lax.rsqrt(tsq[mine, :] + tsq_in[...] + 1e-06)
        weights = []
        for j in range(tiles):
            first = plane * plane_blocks + j * tile_blocks
            row = labels[first]
            total_sq = row[1:2]
            row = row[0:1]
            for i in range(1, tile_blocks):
                more = labels[first + i]
                row = jnp.maximum(row, more[0:1])
                total_sq = total_sq + more[1:2]
            val_hot = (label_ids == row.astype(jnp.int32)).astype(jnp.float32).astype(jnp.bfloat16)
            val_table = jnp.dot(table, val_hot, preferred_element_type=jnp.float32)
            weights.append(
                row_scale
                * lax.rsqrt(total_sq + 1e-06)
                * lax.dot_general(
                    row_hot, val_table.astype(jnp.bfloat16), (((0,), (0,)), ((), ())),
                    preferred_element_type=jnp.float32,
                )
            )
        pair_wait(part_in.at[step], pair_sems.at[step])
        for j in range(tiles):
            cols = pl.ds(j * LANES, LANES)
            weight = weights[j]
            raw = own_part[step, :, cols] + part_in[step, :, cols].astype(jnp.float32)
            place = pl.multiple_of((plane * tiles + j) * LANES, LANES)
            out_ref[:, pl.ds(place, LANES)] = jnp.where(weight != 0.0, raw * weight, 0.0).astype(
                jnp.bfloat16
            )

    column(0)
    val_copy.wait()
    squares = None
    for l in range(lay_dev):
        value = gath[me, l].astype(jnp.float32)
        squares = value * value if squares is None else squares + value * value
    own_sq = lax.dot_general(
        jnp.ones((8, width), jnp.float32), squares, (((1,), (1,)), ((), ())),
        precision=lax.Precision.HIGHEST, preferred_element_type=jnp.float32,
    )
    lane_block = lax.broadcasted_iota(jnp.int32, (1, LANES), 1) // val_dev
    mine_here = lane_block == me % tile_blocks
    vsq[...] = jnp.where(mine_here, jnp.concatenate([own_sq] * tile_blocks, axis=1), 0.0)
    sends.go(vsq, vsq_in, local_sems.at[8], other_core)

    def label_first(_):
        pair_wait(vsq_in, local_sems.at[8])
        own_labels = jnp.concatenate([vpair_ref[...]] * tile_blocks, axis=1)
        labels[me, pl.ds(0, 1)] = jnp.where(mine_here, own_labels, -1).astype(jnp.float32)
        labels[me, pl.ds(1, 1)] = vsq[pl.ds(0, 1), :] + vsq_in[pl.ds(0, 1), :]
        label_start(2)

    train_copy.wait()
    for copy in small_copies:
        copy.wait()

    def last_quarter(start, stop):
        precondition(start, stop)
        sends.go(tsq.at[theirs], tsq_in, local_sems.at[2], other_core)

    def label_mid(_):
        label_line(2)
        label_start(1)

    def label_late(_):
        label_line(1)
        label_start(0)

    def multiply(step):
        third(step)
        product(step)

    quarter = tr_ex // 4
    events = [
        (0.5, lambda _: precondition(0, quarter), 0),
        (1.6, label_first, 0),
        (3.4, lambda _: precondition(quarter, 2 * quarter), 0),
        (3.5, lambda _: precondition(2 * quarter, 3 * quarter), 0),
        (3.6, label_mid, 0),
        (4.5, lambda _: last_quarter(3 * quarter, tr_ex), 0),
        (5.6, label_late, 0),
    ]
    for step in range(z_n):
        if step:
            if relays and step > 1:
                early, late = ((3.0, 6.8), (7.0, 10.6))[step - 2]
                events.append((early, lambda k: column(k, in_middle), step))
                events.append((late, lambda k: column(k, at_end), step))
            else:
                events.append((1.0 + 2.0 * step if step > 1 else 2.9, column, step))
            events.append((7.2 + 1.6 * (step - 1), lambda k: label_take(0, k), step))
        events.append((2.2 + 4.5 * step if step < 2 else 8.5 + step, second, step))
        events.append((7.5 + 2.2 * step if step < 2 else 2.4 * step + 8.1, multiply, step))
    if relays:
        for key, step in ((4.9, 0), (9.6, 1), (10.0, 2), (15.0, 3)):
            events.append((key, relay, step))
    for _, act, step in sorted(events, key=lambda event: event[0]):
        act(step)
        if act is multiply:
            if step == 0:
                pair_wait(tsq_in, local_sems.at[2])
            else:
                finish(step - 1)
    finish(z_n - 1)
    sends.finish()


def solution(mesh):
    box = box_of(mesh.shape["ex"])

    def local(
        train_sketch, val_sketch, first_moment, second_moment, train_pair, val_pair, block_mask
    ):
        lay_dev, tr_ex, width = train_sketch.shape
        val_dev = val_sketch.shape[1]
        ex_n, layer_n = mesh.shape["ex"], mesh.shape["layer"]
        rows = tr_ex // layer_n
        z_n, y_n, x_n = box
        plane_cols = y_n * x_n * val_dev
        scale_factor = float(lay_dev * layer_n * width) ** 0.25
        vmem = pl.BlockSpec(memory_space=pltpu.VMEM)
        hbm = pl.BlockSpec(memory_space=pltpu.HBM)
        scores = pl.pallas_call(
            functools.partial(kernel, box, scale_factor),
            out_shape=jax.ShapeDtypeStruct((rows, ex_n * val_dev), jnp.bfloat16),
            in_specs=[hbm] * 7,
            out_specs=vmem,
            scratch_shapes=[
                pltpu.VMEM(first_moment.shape, jnp.float32),
                pltpu.VMEM(second_moment.shape, jnp.float32),
                pltpu.VMEM((1, tr_ex), jnp.int32),
                pltpu.VMEM((1, val_dev), jnp.int32),
                pltpu.VMEM(block_mask.shape, jnp.int32),
                pltpu.VMEM((ex_n, lay_dev, val_dev, width), jnp.bfloat16),
                pltpu.VMEM((lay_dev, tr_ex, width), jnp.bfloat16),
                pltpu.VMEM((lay_dev, tr_ex, width), jnp.bfloat16),
                pltpu.VMEM((tr_ex, LANES), jnp.float32),
                pltpu.VMEM((rows, LANES), jnp.float32),
                pltpu.VMEM((z_n, rows, plane_cols), jnp.bfloat16),
                pltpu.VMEM((z_n, rows, plane_cols), jnp.bfloat16),
                pltpu.VMEM((z_n, rows, plane_cols), jnp.float32),
                pltpu.VMEM((8, LANES), jnp.float32),
                pltpu.VMEM((8, LANES), jnp.float32),
                pltpu.VMEM((ex_n, 2, LANES), jnp.float32),
                pltpu.SemaphoreType.DMA((9,)),
                pltpu.SemaphoreType.DMA((send_sites(box, z_n),)),
                pltpu.SemaphoreType.DMA((2, ex_n)),
                pltpu.SemaphoreType.DMA((z_n,)),
                pltpu.SemaphoreType.DMA((3, max(box))),
            ],
            compiler_params=pltpu.CompilerParams(
                collective_id=0, has_side_effects=True, vmem_limit_bytes=48 * 1024 * 1024
            ),
        )(
            *(
                pltpu.with_memory_space_constraint(array, pltpu.HBM)
                for array in (
                    train_sketch, val_sketch, first_moment, second_moment,
                    train_pair[None, :], val_pair[None, :], block_mask,
                )
            )
        )
        return scores[:, None, :]

    placed = (
        P("layer", "ex", None),
        P("layer", "ex", None),
        P("layer", None),
        P("layer", None),
        P("ex"),
        P("ex"),
        P(),
    )
    return jax.shard_map(
        local, mesh=mesh, in_specs=placed, out_specs=P("ex", "layer", None), check_vma=False
    )
```

```python
import functools

import jax
import jax.numpy as jnp
from jax import lax
from jax.experimental import pallas as pl
from jax.experimental.pallas import tpu as pltpu
from jax.sharding import PartitionSpec as P

MESH = pl.DeviceIdType.MESH
LANES = 128
CHUNK = 32


def box_of(count):
    side = 1
    while (side * 2) ** 3 * 2 <= count and count % ((side * 2) ** 2) == 0:
        side *= 2
    return count // (side * side), side, side


def visit(here, extent, step):
    if step == 0:
        return here
    below, above = here, extent - 1 - here
    least = jnp.minimum(below, above)
    away = jnp.where(below < above, 1, -1)
    near = here + away * ((step + 1) // 2 if step % 2 else -(step // 2))
    return jnp.where(step <= 2 * least, near, here + away * (step - least))


class Sends:
    def __init__(self, sems):
        self.sems = sems
        self.made = []

    def go(self, src, dst, recv_sem, target, cond=None):
        index = len(self.made)

        def make():
            return pltpu.make_async_remote_copy(
                src_ref=src,
                dst_ref=dst,
                send_sem=self.sems.at[index],
                recv_sem=recv_sem,
                device_id=target,
                device_id_type=MESH,
            )

        self.made.append((make, cond))
        if cond is None:
            make().start()
        else:
            pl.when(cond)(lambda: make().start())

    def finish(self):
        for make, cond in self.made:
            if cond is None:
                make().wait_send()
            else:
                pl.when(cond)(lambda make=make: make().wait_send())


def send_sites(box, planes):
    z_n, y_n, x_n = box
    line = lambda n: 0 if n == 1 else 1 if n == 2 else 2 + (n - 1)
    per = 2 + 2 * (line(y_n) + line(x_n) + y_n * line(x_n) + x_n * line(y_n))
    return z_n * (per + 4) + 32 + 2 * z_n + 3 * (z_n + y_n + x_n)


def kernel(
    box, scale_factor,
    train_hbm, val_hbm, first_hbm, second_hbm, tpair_hbm, vpair_hbm, mask_hbm,
    out_ref,
    first_ref, second_ref, tpair_ref, vpair_ref, mask_ref,
    gath, train, pre, tsq, tsq_in, part_out, part_in, own_part, vsq, vsq_in, labels,
    local_sems, send_sems, block_sems, pair_sems, label_sems,
):
    z_n, y_n, x_n = box
    plane_blocks = y_n * x_n
    lay_dev, tr_ex, width = train.shape
    val_dev = gath.shape[2]
    half = lay_dev // 2
    rows = out_ref.shape[0]
    tile_blocks = LANES // val_dev
    tiles = plane_blocks // tile_blocks
    pair_count = mask_ref.shape[0]
    core = lax.axis_index("layer")
    me = lax.axis_index("ex")
    z, y, x = me // plane_blocks, (me // x_n) % y_n, me % x_n
    slot = lambda a, b, c: (a * y_n + b) * x_n + c
    at_ex = lambda a, b, c: {"ex": slot(a, b, c)}
    other_core = {"layer": 1 - core}
    sends = Sends(send_sems)

    train_copy = pltpu.make_async_copy(train_hbm, train, local_sems.at[0])
    train_copy.start()
    val_copy = pltpu.make_async_copy(val_hbm, gath.at[me], local_sems.at[1])
    val_copy.start()
    small_copies = [
        pltpu.make_async_copy(src, dst, local_sems.at[3 + i])
        for i, (src, dst) in enumerate(
            (
                (vpair_hbm, vpair_ref),
                (first_hbm, first_ref),
                (second_hbm, second_ref),
                (tpair_hbm, tpair_ref),
                (mask_hbm, mask_ref),
            )
        )
    ]
    for copy in small_copies:
        copy.start()

    def neighbours(dim):
        here, extent = ((z, z_n), (y, y_n), (x, x_n))[dim]

        def device(pos):
            return at_ex(*(pos if d == dim else c for d, c in enumerate((z, y, x))))

        if extent == 1:
            return []
        if extent == 2:
            return [(device(1 - here), None)]
        return [(device(here + 1), here < extent - 1), (device(here - 1), here > 0)]

    def onward(dim, came_from):
        here, extent = ((z, z_n), (y, y_n), (x, x_n))[dim]
        if extent <= 2:
            return []
        pos = jnp.where(came_from < here, here + 1, here - 1)
        device = at_ex(*(pos if d == dim else c for d, c in enumerate((z, y, x))))
        return [(device, jnp.logical_and(pos >= 0, pos < extent))]

    relays = box == (4, 2, 2)
    at_end = jnp.logical_or(z == 0, z == z_n - 1)
    in_middle = jnp.logical_and(z > 0, z < z_n - 1)

    barrier = pltpu.get_barrier_semaphore()
    pl.semaphore_signal(barrier, inc=1, device_id=other_core, device_id_type=MESH)
    expected = 1
    for dim in range(3):
        for device, cond in neighbours(dim):
            def greet(device=device):
                pl.semaphore_signal(barrier, inc=1, device_id=device, device_id_type=MESH)

            if cond is None:
                greet()
                expected = expected + 1
            else:
                pl.when(cond)(greet)
                expected = expected + jnp.where(cond, 1, 0)
    if relays:
        @pl.when(at_end)
        def _():
            pl.semaphore_signal(
                barrier, inc=1, device_id=at_ex(z_n - 1 - z, y, x), device_id_type=MESH
            )

        expected = expected + jnp.where(at_end, 1, 0)
    pl.semaphore_wait(barrier, expected)

    def block(h, where):
        return gath.at[where, pl.ds(h * half, half)]

    def send_block(h, where, targets, own=False):
        src = val_hbm.at[pl.ds(h * half, half)] if own else block(h, where)
        for device, cond in targets:
            sends.go(src, block(h, where), block_sems.at[h, where], device, cond)

    def wait_block(h, where):
        pltpu.make_async_copy(block(h, where), block(h, where), block_sems.at[h, where]).wait()

    order = ((1, 2), (2, 1))

    def column(step):
        plane = visit(z, z_n, step)
        where = slot(plane, y, x)
        for h in (0, 1):
            if step:
                wait_block(h, where)
                if not (relays and step == z_n - 1):
                    send_block(h, where, onward(0, plane))
            else:
                send_block(h, where, neighbours(0), True)
            send_block(h, where, neighbours(order[h][0]), not step)
        for h in (0, 1):
            send_block(h, where, neighbours(order[h][1]), not step)
        if relays and not step:
            for h in (0, 1):
                send_block(h, where, [(at_ex(z_n - 1 - z, y, x), at_end)], True)

    def second(step):
        plane = visit(z, z_n, step)
        for h in (0, 1):
            dim, last = order[h]
            here, extent = ((z, z_n), (y, y_n), (x, x_n))[dim]
            for k in range(1, extent):
                pos = visit(here, extent, k)
                where = slot(plane, pos, x) if dim == 1 else slot(plane, y, pos)
                wait_block(h, where)
                send_block(h, where, onward(dim, pos))
                if not relays:
                    send_block(h, where, neighbours(last))
                elif step != 2:
                    cond = (None, in_middle, None, at_end)[step]
                    send_block(h, where, [(device, cond) for device, _ in neighbours(last)])

    def relay(step):
        where = slot(visit(z, z_n, step), 1 - y, 1 - x)
        pair = z + 1 - 2 * (z % 2)
        target = at_ex(z_n - 1 - z if step == 2 else pair, y, x)
        cond = in_middle if step else None
        for h in (0, 1):
            if step == 2:
                pl.when(in_middle)(lambda h=h: wait_block(h, where))
            else:
                wait_block(h, where)
            if step < 3:
                send_block(h, where, [(target, cond)])

    def third(step):
        plane = visit(z, z_n, step)
        if relays:
            for h in (0, 1):
                wait_block(h, slot(plane, y, 1 - x) if h == 0 else slot(plane, 1 - y, x))
                if step == 2:
                    where = slot(plane, 1 - y, 1 - x)
                    pl.when(at_end)(lambda h=h, where=where: wait_block(h, where))
            return
        for h in (0, 1):
            dim, last = order[h]
            here, extent = ((z, z_n), (y, y_n), (x, x_n))[dim]
            here_last, extent_last = ((z, z_n), (y, y_n), (x, x_n))[last]
            for k in range(extent):
                pos = visit(here, extent, k)
                for m in range(1, extent_last):
                    end = visit(here_last, extent_last, m)
                    where = slot(plane, pos, end) if dim == 1 else slot(plane, end, pos)
                    wait_block(h, where)
                    send_block(h, where, onward(last, end))

    def label_group(dim, pos):
        if dim == 2:
            return labels.at[pl.ds(slot(z, y, pos), 1)]
        if dim == 1:
            return labels.at[pl.ds(slot(z, pos, 0), x_n)]
        return labels.at[pl.ds(slot(pos, 0, 0), plane_blocks)]

    def send_labels(dim, pos, targets):
        for device, cond in targets:
            sends.go(
                label_group(dim, pos), label_group(dim, pos), label_sems.at[dim, pos], device, cond
            )

    def label_start(dim):
        send_labels(dim, (z, y, x)[dim], neighbours(dim))

    def label_take(dim, step):
        here, extent = ((z, z_n), (y, y_n), (x, x_n))[dim]
        pos = visit(here, extent, step)
        group = label_group(dim, pos)
        pltpu.make_async_copy(group, group, label_sems.at[dim, pos]).wait()
        send_labels(dim, pos, onward(dim, pos))

    def label_line(dim):
        for k in range(1, (z_n, y_n, x_n)[dim]):
            label_take(dim, k)

    def precondition(start, stop):
        @pl.loop(start // CHUNK, stop // CHUNK)
        def _(c):
            here = pl.ds(pl.multiple_of(c * CHUNK, CHUNK), CHUNK)
            total = jnp.zeros((CHUNK, width), jnp.float32)
            for l in range(lay_dev):
                grad = train[l, here, :].astype(jnp.float32)
                first = first_ref[pl.ds(l, 1), :] * 0.9
                second_m = second_ref[pl.ds(l, 1), :] * 0.999
                spread = second_m + 0.001 * grad * grad
                root = lax.rsqrt(spread)
                more = 1.0 + 1e-08 * root
                value = (first + 0.1 * grad) * lax.rsqrt(spread * more * more)
                total = total + value * value
                pre[l, here, :] = value.astype(jnp.bfloat16)
            tsq[here, :] = jnp.broadcast_to(jnp.sum(total, axis=1, keepdims=True), (CHUNK, LANES))

    mine = pl.ds(pl.multiple_of(core * rows, rows), rows)
    theirs = pl.ds(pl.multiple_of((1 - core) * rows, rows), rows)

    def product(step):
        plane = visit(z, z_n, step)
        for j in range(tiles):
            cols = pl.ds(j * LANES, LANES)
            blocks = pl.ds(plane * plane_blocks + j * tile_blocks, tile_blocks)
            layer = lambda l: gath[blocks, l].reshape(LANES, width)

            def dot(where):
                total = None
                for l in range(lay_dev):
                    term = lax.dot_general(
                        pre[l, where, :], layer(l), (((1,), (1,)), ((), ())),
                        preferred_element_type=jnp.float32,
                    )
                    total = term if total is None else total + term
                return total

            part_out[step, :, cols] = dot(theirs).astype(jnp.bfloat16)
            if j == tiles - 1:
                sends.go(part_out.at[step], part_in.at[step], pair_sems.at[step], other_core)
            own_part[step, :, cols] = dot(mine)

    def pair_wait(buffer, sem):
        pltpu.make_async_copy(buffer, buffer, sem).wait()

    def finish(step):
        plane = visit(z, z_n, step)
        pair_ids = lax.broadcasted_iota(jnp.int32, (pair_count, rows), 0)
        row_hot = (pair_ids == tpair_ref[:, mine]).astype(jnp.float32).astype(jnp.bfloat16)
        table = mask_ref[...].astype(jnp.float32).astype(jnp.bfloat16)
        label_ids = lax.broadcasted_iota(jnp.int32, (pair_count, LANES), 0)
        row_scale = (scale_factor * scale_factor) * lax.rsqrt(tsq[mine, :] + tsq_in[...] + 1e-06)
        weights = []
        for j in range(tiles):
            first = plane * plane_blocks + j * tile_blocks
            row = labels[first]
            total_sq = row[1:2]
            row = row[0:1]
            for i in range(1, tile_blocks):
                more = labels[first + i]
                row = jnp.maximum(row, more[0:1])
                total_sq = total_sq + more[1:2]
            val_hot = (label_ids == row.astype(jnp.int32)).astype(jnp.float32).astype(jnp.bfloat16)
            val_table = jnp.dot(table, val_hot, preferred_element_type=jnp.float32)
            weights.append(
                row_scale
                * lax.rsqrt(total_sq + 1e-06)
                * lax.dot_general(
                    row_hot, val_table.astype(jnp.bfloat16), (((0,), (0,)), ((), ())),
                    preferred_element_type=jnp.float32,
                )
            )
        pair_wait(part_in.at[step], pair_sems.at[step])
        for j in range(tiles):
            cols = pl.ds(j * LANES, LANES)
            weight = weights[j]
            raw = own_part[step, :, cols] + part_in[step, :, cols].astype(jnp.float32)
            place = pl.multiple_of((plane * tiles + j) * LANES, LANES)
            out_ref[:, pl.ds(place, LANES)] = jnp.where(weight != 0.0, raw * weight, 0.0).astype(
                jnp.bfloat16
            )

    column(0)
    val_copy.wait()
    squares = None
    for l in range(lay_dev):
        value = gath[me, l].astype(jnp.float32)
        squares = value * value if squares is None else squares + value * value
    own_sq = lax.dot_general(
        jnp.ones((8, width), jnp.float32), squares, (((1,), (1,)), ((), ())),
        precision=lax.Precision.HIGHEST, preferred_element_type=jnp.float32,
    )
    lane_block = lax.broadcasted_iota(jnp.int32, (1, LANES), 1) // val_dev
    mine_here = lane_block == me % tile_blocks
    vsq[...] = jnp.where(mine_here, jnp.concatenate([own_sq] * tile_blocks, axis=1), 0.0)
    sends.go(vsq, vsq_in, local_sems.at[8], other_core)

    def label_first(_):
        pair_wait(vsq_in, local_sems.at[8])
        own_labels = jnp.concatenate([vpair_ref[...]] * tile_blocks, axis=1)
        labels[me, pl.ds(0, 1)] = jnp.where(mine_here, own_labels, -1).astype(jnp.float32)
        labels[me, pl.ds(1, 1)] = vsq[pl.ds(0, 1), :] + vsq_in[pl.ds(0, 1), :]
        label_start(2)

    train_copy.wait()
    for copy in small_copies:
        copy.wait()

    def last_quarter(start, stop):
        precondition(start, stop)
        sends.go(tsq.at[theirs], tsq_in, local_sems.at[2], other_core)

    def label_mid(_):
        label_line(2)
        label_start(1)

    def label_late(_):
        label_line(1)
        label_start(0)

    def multiply(step):
        third(step)
        product(step)

    quarter = tr_ex // 4
    events = [
        (0.5, lambda _: precondition(0, quarter), 0),
        (1.6, label_first, 0),
        (3.4, lambda _: precondition(quarter, 2 * quarter), 0),
        (3.5, lambda _: precondition(2 * quarter, 3 * quarter), 0),
        (3.6, label_mid, 0),
        (4.5, lambda _: last_quarter(3 * quarter, tr_ex), 0),
        (5.6, label_late, 0),
    ]
    for step in range(z_n):
        if step:
            events.append((2.2 * step - 1.3 if step > 1 else 2.9, column, step))
            events.append((7.2 + 1.6 * (step - 1), lambda k: label_take(0, k), step))
        events.append((2.2 + 4.5 * step if step < 2 else 8.5 + step, second, step))
        events.append((7.5 + 2.2 * step if step < 2 else 2.4 * step + 8.1, multiply, step))
    if relays:
        for key, step in ((4.9, 0), (9.0, 1), (10.0, 2), (15.0, 3)):
            events.append((key, relay, step))
    for _, act, step in sorted(events, key=lambda event: event[0]):
        act(step)
        if act is multiply:
            if step == 0:
                pair_wait(tsq_in, local_sems.at[2])
            else:
                finish(step - 1)
    finish(z_n - 1)
    sends.finish()


def solution(mesh):
    box = box_of(mesh.shape["ex"])

    def local(
        train_sketch, val_sketch, first_moment, second_moment, train_pair, val_pair, block_mask
    ):
        lay_dev, tr_ex, width = train_sketch.shape
        val_dev = val_sketch.shape[1]
        ex_n, layer_n = mesh.shape["ex"], mesh.shape["layer"]
        rows = tr_ex // layer_n
        z_n, y_n, x_n = box
        plane_cols = y_n * x_n * val_dev
        scale_factor = float(lay_dev * layer_n * width) ** 0.25
        vmem = pl.BlockSpec(memory_space=pltpu.VMEM)
        hbm = pl.BlockSpec(memory_space=pltpu.HBM)
        scores = pl.pallas_call(
            functools.partial(kernel, box, scale_factor),
            out_shape=jax.ShapeDtypeStruct((rows, ex_n * val_dev), jnp.bfloat16),
            in_specs=[hbm] * 7,
            out_specs=vmem,
            scratch_shapes=[
                pltpu.VMEM(first_moment.shape, jnp.float32),
                pltpu.VMEM(second_moment.shape, jnp.float32),
                pltpu.VMEM((1, tr_ex), jnp.int32),
                pltpu.VMEM((1, val_dev), jnp.int32),
                pltpu.VMEM(block_mask.shape, jnp.int32),
                pltpu.VMEM((ex_n, lay_dev, val_dev, width), jnp.bfloat16),
                pltpu.VMEM((lay_dev, tr_ex, width), jnp.bfloat16),
                pltpu.VMEM((lay_dev, tr_ex, width), jnp.bfloat16),
                pltpu.VMEM((tr_ex, LANES), jnp.float32),
                pltpu.VMEM((rows, LANES), jnp.float32),
                pltpu.VMEM((z_n, rows, plane_cols), jnp.bfloat16),
                pltpu.VMEM((z_n, rows, plane_cols), jnp.bfloat16),
                pltpu.VMEM((z_n, rows, plane_cols), jnp.float32),
                pltpu.VMEM((8, LANES), jnp.float32),
                pltpu.VMEM((8, LANES), jnp.float32),
                pltpu.VMEM((ex_n, 2, LANES), jnp.float32),
                pltpu.SemaphoreType.DMA((9,)),
                pltpu.SemaphoreType.DMA((send_sites(box, z_n),)),
                pltpu.SemaphoreType.DMA((2, ex_n)),
                pltpu.SemaphoreType.DMA((z_n,)),
                pltpu.SemaphoreType.DMA((3, max(box))),
            ],
            compiler_params=pltpu.CompilerParams(
                collective_id=0, has_side_effects=True, vmem_limit_bytes=48 * 1024 * 1024
            ),
        )(
            *(
                pltpu.with_memory_space_constraint(array, pltpu.HBM)
                for array in (
                    train_sketch, val_sketch, first_moment, second_moment,
                    train_pair[None, :], val_pair[None, :], block_mask,
                )
            )
        )
        return scores[:, None, :]

    placed = (
        P("layer", "ex", None),
        P("layer", "ex", None),
        P("layer", None),
        P("layer", None),
        P("ex"),
        P("ex"),
        P(),
    )
    return jax.shard_map(
        local, mesh=mesh, in_specs=placed, out_specs=P("ex", "layer", None), check_vma=False
    )
```

```python
import functools

import jax
import jax.numpy as jnp
from jax import lax
from jax.experimental import pallas as pl
from jax.experimental.pallas import tpu as pltpu
from jax.sharding import PartitionSpec as P

MESH = pl.DeviceIdType.MESH
LANES = 128
CHUNK = 32


def box_of(count):
    side = 1
    while (side * 2) ** 3 * 2 <= count and count % ((side * 2) ** 2) == 0:
        side *= 2
    return count // (side * side), side, side


def visit(here, extent, step):
    if step == 0:
        return here
    below, above = here, extent - 1 - here
    least = jnp.minimum(below, above)
    away = jnp.where(below < above, 1, -1)
    near = here + away * ((step + 1) // 2 if step % 2 else -(step // 2))
    return jnp.where(step <= 2 * least, near, here + away * (step - least))


class Sends:
    def __init__(self, sems):
        self.sems = sems
        self.made = []

    def go(self, src, dst, recv_sem, target, cond=None):
        index = len(self.made)

        def make():
            return pltpu.make_async_remote_copy(
                src_ref=src,
                dst_ref=dst,
                send_sem=self.sems.at[index],
                recv_sem=recv_sem,
                device_id=target,
                device_id_type=MESH,
            )

        self.made.append((make, cond))
        if cond is None:
            make().start()
        else:
            pl.when(cond)(lambda: make().start())

    def finish(self):
        for make, cond in self.made:
            if cond is None:
                make().wait_send()
            else:
                pl.when(cond)(lambda make=make: make().wait_send())


def send_sites(box, planes):
    z_n, y_n, x_n = box
    line = lambda n: 0 if n == 1 else 1 if n == 2 else 2 + (n - 1)
    per = 2 + 2 * (line(y_n) + line(x_n) + y_n * line(x_n) + x_n * line(y_n))
    return z_n * (per + 4) + 16 + 2 * z_n + 3 * (z_n + y_n + x_n)


def kernel(
    box, scale_factor,
    train_hbm, val_hbm, first_hbm, second_hbm, tpair_hbm, vpair_hbm, mask_hbm,
    out_ref,
    first_ref, second_ref, tpair_ref, vpair_ref, mask_ref,
    gath, train, pre, tsq, tsq_in, part_out, part_in, own_part, vsq, vsq_in, labels,
    local_sems, send_sems, block_sems, pair_sems, label_sems,
):
    z_n, y_n, x_n = box
    plane_blocks = y_n * x_n
    lay_dev, tr_ex, width = train.shape
    val_dev = gath.shape[2]
    half = lay_dev // 2
    rows = out_ref.shape[0]
    tile_blocks = LANES // val_dev
    tiles = plane_blocks // tile_blocks
    pair_count = mask_ref.shape[0]
    core = lax.axis_index("layer")
    me = lax.axis_index("ex")
    z, y, x = me // plane_blocks, (me // x_n) % y_n, me % x_n
    slot = lambda a, b, c: (a * y_n + b) * x_n + c
    at_ex = lambda a, b, c: {"ex": slot(a, b, c)}
    other_core = {"layer": 1 - core}
    sends = Sends(send_sems)

    train_copy = pltpu.make_async_copy(train_hbm, train, local_sems.at[0])
    train_copy.start()
    val_copy = pltpu.make_async_copy(val_hbm, gath.at[me], local_sems.at[1])
    val_copy.start()
    small_copies = [
        pltpu.make_async_copy(src, dst, local_sems.at[3 + i])
        for i, (src, dst) in enumerate(
            (
                (vpair_hbm, vpair_ref),
                (first_hbm, first_ref),
                (second_hbm, second_ref),
                (tpair_hbm, tpair_ref),
                (mask_hbm, mask_ref),
            )
        )
    ]
    for copy in small_copies:
        copy.start()

    def neighbours(dim):
        here, extent = ((z, z_n), (y, y_n), (x, x_n))[dim]

        def device(pos):
            return at_ex(*(pos if d == dim else c for d, c in enumerate((z, y, x))))

        if extent == 1:
            return []
        if dim == 0:
            return [(device(visit(here, extent, k)), None) for k in range(1, extent)]
        if extent == 2:
            return [(device(1 - here), None)]
        return [(device(here + 1), here < extent - 1), (device(here - 1), here > 0)]

    def onward(dim, came_from):
        here, extent = ((z, z_n), (y, y_n), (x, x_n))[dim]
        if extent <= 2 or dim == 0:
            return []
        pos = jnp.where(came_from < here, here + 1, here - 1)
        device = at_ex(*(pos if d == dim else c for d, c in enumerate((z, y, x))))
        return [(device, jnp.logical_and(pos >= 0, pos < extent))]

    barrier = pltpu.get_barrier_semaphore()
    pl.semaphore_signal(barrier, inc=1, device_id=other_core, device_id_type=MESH)
    expected = 1
    for dim in range(3):
        for device, cond in neighbours(dim):
            def greet(device=device):
                pl.semaphore_signal(barrier, inc=1, device_id=device, device_id_type=MESH)

            if cond is None:
                greet()
                expected = expected + 1
            else:
                pl.when(cond)(greet)
                expected = expected + jnp.where(cond, 1, 0)
    pl.semaphore_wait(barrier, expected)

    def block(h, where):
        return gath.at[where, pl.ds(h * half, half)]

    def send_block(h, where, targets, own=False):
        src = val_hbm.at[pl.ds(h * half, half)] if own else block(h, where)
        for device, cond in targets:
            sends.go(src, block(h, where), block_sems.at[h, where], device, cond)

    def wait_block(h, where):
        pltpu.make_async_copy(block(h, where), block(h, where), block_sems.at[h, where]).wait()

    order = ((1, 2), (2, 1))

    def column(step):
        plane = visit(z, z_n, step)
        where = slot(plane, y, x)
        for h in (0, 1):
            if step:
                wait_block(h, where)
            send_block(h, where, neighbours(order[h][0]), not step)
        if not step:
            for target in neighbours(0)[:1]:
                for h in (0, 1):
                    send_block(h, where, [target], True)
        for h in (0, 1):
            send_block(h, where, neighbours(order[h][1]), not step)
        if not step:
            for target in neighbours(0)[1:]:
                for h in (0, 1):
                    send_block(h, where, [target], True)

    def second(step):
        plane = visit(z, z_n, step)
        for h in (0, 1):
            dim, last = order[h]
            here, extent = ((z, z_n), (y, y_n), (x, x_n))[dim]
            for k in range(1, extent):
                pos = visit(here, extent, k)
                where = slot(plane, pos, x) if dim == 1 else slot(plane, y, pos)
                wait_block(h, where)
                send_block(h, where, onward(dim, pos))
                send_block(h, where, neighbours(last))

    def third(step):
        plane = visit(z, z_n, step)
        for h in (0, 1):
            dim, last = order[h]
            here, extent = ((z, z_n), (y, y_n), (x, x_n))[dim]
            here_last, extent_last = ((z, z_n), (y, y_n), (x, x_n))[last]
            for k in range(extent):
                pos = visit(here, extent, k)
                for m in range(1, extent_last):
                    end = visit(here_last, extent_last, m)
                    where = slot(plane, pos, end) if dim == 1 else slot(plane, end, pos)
                    wait_block(h, where)
                    send_block(h, where, onward(last, end))

    def label_group(dim, pos):
        if dim == 2:
            return labels.at[pl.ds(slot(z, y, pos), 1)]
        if dim == 1:
            return labels.at[pl.ds(slot(z, pos, 0), x_n)]
        return labels.at[pl.ds(slot(pos, 0, 0), plane_blocks)]

    def send_labels(dim, pos, targets):
        for device, cond in targets:
            sends.go(
                label_group(dim, pos), label_group(dim, pos), label_sems.at[dim, pos], device, cond
            )

    def label_start(dim):
        send_labels(dim, (z, y, x)[dim], neighbours(dim))

    def label_take(dim, step):
        here, extent = ((z, z_n), (y, y_n), (x, x_n))[dim]
        pos = visit(here, extent, step)
        group = label_group(dim, pos)
        pltpu.make_async_copy(group, group, label_sems.at[dim, pos]).wait()
        send_labels(dim, pos, onward(dim, pos))

    def label_line(dim):
        for k in range(1, (z_n, y_n, x_n)[dim]):
            label_take(dim, k)

    def precondition(start, stop):
        @pl.loop(start // CHUNK, stop // CHUNK)
        def _(c):
            here = pl.ds(pl.multiple_of(c * CHUNK, CHUNK), CHUNK)
            total = jnp.zeros((CHUNK, width), jnp.float32)
            for l in range(lay_dev):
                grad = train[l, here, :].astype(jnp.float32)
                first = first_ref[pl.ds(l, 1), :] * 0.9
                second_m = second_ref[pl.ds(l, 1), :] * 0.999
                spread = second_m + 0.001 * grad * grad
                root = lax.rsqrt(spread)
                more = 1.0 + 1e-08 * root
                value = (first + 0.1 * grad) * lax.rsqrt(spread * more * more)
                total = total + value * value
                pre[l, here, :] = value.astype(jnp.bfloat16)
            tsq[here, :] = jnp.broadcast_to(jnp.sum(total, axis=1, keepdims=True), (CHUNK, LANES))

    mine = pl.ds(pl.multiple_of(core * rows, rows), rows)
    theirs = pl.ds(pl.multiple_of((1 - core) * rows, rows), rows)

    def product(step):
        plane = visit(z, z_n, step)
        for j in range(tiles):
            cols = pl.ds(j * LANES, LANES)
            blocks = pl.ds(plane * plane_blocks + j * tile_blocks, tile_blocks)
            layer = lambda l: gath[blocks, l].reshape(LANES, width)

            def dot(where):
                total = None
                for l in range(lay_dev):
                    term = lax.dot_general(
                        pre[l, where, :], layer(l), (((1,), (1,)), ((), ())),
                        preferred_element_type=jnp.float32,
                    )
                    total = term if total is None else total + term
                return total

            part_out[step, :, cols] = dot(theirs).astype(jnp.bfloat16)
            if j == tiles - 1:
                sends.go(part_out.at[step], part_in.at[step], pair_sems.at[step], other_core)
            own_part[step, :, cols] = dot(mine)

    def pair_wait(buffer, sem):
        pltpu.make_async_copy(buffer, buffer, sem).wait()

    def finish(step):
        plane = visit(z, z_n, step)
        pair_ids = lax.broadcasted_iota(jnp.int32, (pair_count, rows), 0)
        row_hot = (pair_ids == tpair_ref[:, mine]).astype(jnp.float32).astype(jnp.bfloat16)
        table = mask_ref[...].astype(jnp.float32).astype(jnp.bfloat16)
        label_ids = lax.broadcasted_iota(jnp.int32, (pair_count, LANES), 0)
        row_scale = (scale_factor * scale_factor) * lax.rsqrt(tsq[mine, :] + tsq_in[...] + 1e-06)
        weights = []
        for j in range(tiles):
            first = plane * plane_blocks + j * tile_blocks
            row = labels[first]
            total_sq = row[1:2]
            row = row[0:1]
            for i in range(1, tile_blocks):
                more = labels[first + i]
                row = jnp.maximum(row, more[0:1])
                total_sq = total_sq + more[1:2]
            val_hot = (label_ids == row.astype(jnp.int32)).astype(jnp.float32).astype(jnp.bfloat16)
            val_table = jnp.dot(table, val_hot, preferred_element_type=jnp.float32)
            weights.append(
                row_scale
                * lax.rsqrt(total_sq + 1e-06)
                * lax.dot_general(
                    row_hot, val_table.astype(jnp.bfloat16), (((0,), (0,)), ((), ())),
                    preferred_element_type=jnp.float32,
                )
            )
        pair_wait(part_in.at[step], pair_sems.at[step])
        for j in range(tiles):
            cols = pl.ds(j * LANES, LANES)
            weight = weights[j]
            raw = own_part[step, :, cols] + part_in[step, :, cols].astype(jnp.float32)
            place = pl.multiple_of((plane * tiles + j) * LANES, LANES)
            out_ref[:, pl.ds(place, LANES)] = jnp.where(weight != 0.0, raw * weight, 0.0).astype(
                jnp.bfloat16
            )

    column(0)
    val_copy.wait()
    squares = None
    for l in range(lay_dev):
        value = gath[me, l].astype(jnp.float32)
        squares = value * value if squares is None else squares + value * value
    own_sq = lax.dot_general(
        jnp.ones((8, width), jnp.float32), squares, (((1,), (1,)), ((), ())),
        precision=lax.Precision.HIGHEST, preferred_element_type=jnp.float32,
    )
    lane_block = lax.broadcasted_iota(jnp.int32, (1, LANES), 1) // val_dev
    mine_here = lane_block == me % tile_blocks
    vsq[...] = jnp.where(mine_here, jnp.concatenate([own_sq] * tile_blocks, axis=1), 0.0)
    sends.go(vsq, vsq_in, local_sems.at[8], other_core)

    def label_first(_):
        pair_wait(vsq_in, local_sems.at[8])
        own_labels = jnp.concatenate([vpair_ref[...]] * tile_blocks, axis=1)
        labels[me, pl.ds(0, 1)] = jnp.where(mine_here, own_labels, -1).astype(jnp.float32)
        labels[me, pl.ds(1, 1)] = vsq[pl.ds(0, 1), :] + vsq_in[pl.ds(0, 1), :]
        label_start(2)

    train_copy.wait()
    for copy in small_copies:
        copy.wait()

    def last_quarter(start, stop):
        precondition(start, stop)
        sends.go(tsq.at[theirs], tsq_in, local_sems.at[2], other_core)

    def label_mid(_):
        label_line(2)
        label_start(1)

    def label_late(_):
        label_line(1)
        label_start(0)

    def multiply(step):
        third(step)
        product(step)

    quarter = tr_ex // 4
    events = [
        (0.5, lambda _: precondition(0, quarter), 0),
        (1.6, label_first, 0),
        (3.4, label_mid, 0),
        (2.5, lambda _: precondition(quarter, 2 * quarter), 0),
        (5.6, label_late, 0),
        (4.5, lambda _: precondition(2 * quarter, 3 * quarter), 0),
        (5.0, lambda _: last_quarter(3 * quarter, tr_ex), 0),
    ]
    for step in range(z_n):
        if step:
            events.append((2.0 * step - (0.0 if step < 2 else 0.5), column, step))
            events.append((3.0 * step + 4.8, lambda k: label_take(0, k), step))
        events.append((3.0 * step + 1.7, second, step))
        events.append((3.0 * step + 4.9 if step else 7.75, multiply, step))
    for _, act, step in sorted(events, key=lambda event: event[0]):
        act(step)
        if act is multiply:
            if step == 0:
                pair_wait(tsq_in, local_sems.at[2])
            else:
                finish(step - 1)
    finish(z_n - 1)
    sends.finish()


def solution(mesh):
    box = box_of(mesh.shape["ex"])

    def local(
        train_sketch, val_sketch, first_moment, second_moment, train_pair, val_pair, block_mask
    ):
        lay_dev, tr_ex, width = train_sketch.shape
        val_dev = val_sketch.shape[1]
        ex_n, layer_n = mesh.shape["ex"], mesh.shape["layer"]
        rows = tr_ex // layer_n
        z_n, y_n, x_n = box
        plane_cols = y_n * x_n * val_dev
        scale_factor = float(lay_dev * layer_n * width) ** 0.25
        vmem = pl.BlockSpec(memory_space=pltpu.VMEM)
        hbm = pl.BlockSpec(memory_space=pltpu.HBM)
        scores = pl.pallas_call(
            functools.partial(kernel, box, scale_factor),
            out_shape=jax.ShapeDtypeStruct((rows, ex_n * val_dev), jnp.bfloat16),
            in_specs=[hbm] * 7,
            out_specs=vmem,
            scratch_shapes=[
                pltpu.VMEM(first_moment.shape, jnp.float32),
                pltpu.VMEM(second_moment.shape, jnp.float32),
                pltpu.VMEM((1, tr_ex), jnp.int32),
                pltpu.VMEM((1, val_dev), jnp.int32),
                pltpu.VMEM(block_mask.shape, jnp.int32),
                pltpu.VMEM((ex_n, lay_dev, val_dev, width), jnp.bfloat16),
                pltpu.VMEM((lay_dev, tr_ex, width), jnp.bfloat16),
                pltpu.VMEM((lay_dev, tr_ex, width), jnp.bfloat16),
                pltpu.VMEM((tr_ex, LANES), jnp.float32),
                pltpu.VMEM((rows, LANES), jnp.float32),
                pltpu.VMEM((z_n, rows, plane_cols), jnp.bfloat16),
                pltpu.VMEM((z_n, rows, plane_cols), jnp.bfloat16),
                pltpu.VMEM((z_n, rows, plane_cols), jnp.float32),
                pltpu.VMEM((8, LANES), jnp.float32),
                pltpu.VMEM((8, LANES), jnp.float32),
                pltpu.VMEM((ex_n, 2, LANES), jnp.float32),
                pltpu.SemaphoreType.DMA((9,)),
                pltpu.SemaphoreType.DMA((send_sites(box, z_n),)),
                pltpu.SemaphoreType.DMA((2, ex_n)),
                pltpu.SemaphoreType.DMA((z_n,)),
                pltpu.SemaphoreType.DMA((3, max(box))),
            ],
            compiler_params=pltpu.CompilerParams(
                collective_id=0, has_side_effects=True, vmem_limit_bytes=48 * 1024 * 1024
            ),
        )(
            *(
                pltpu.with_memory_space_constraint(array, pltpu.HBM)
                for array in (
                    train_sketch, val_sketch, first_moment, second_moment,
                    train_pair[None, :], val_pair[None, :], block_mask,
                )
            )
        )
        return scores[:, None, :]

    placed = (
        P("layer", "ex", None),
        P("layer", "ex", None),
        P("layer", None),
        P("layer", None),
        P("ex"),
        P("ex"),
        P(),
    )
    return jax.shard_map(
        local, mesh=mesh, in_specs=placed, out_specs=P("ex", "layer", None), check_vma=False
    )
```
